256 devices in a mesh: batch: 4 (over x), seq: 64 (over z, y, core).
Axes of the slice: x: 4, y: 4, z: 8, core: 2. Of those that a mesh axis runs over, the one named last changes fastest.
Arguments:
- tokens: bfloat16 [4, 32768, 1024], P('batch', 'seq'), may hold values from -20 to 20
- slot_parameters: bfloat16 [1024, 256], replicated, may hold values from -0.3125 to 0.3125
- w_in: bfloat16 [128, 1024, 4096], P('seq', None, 'batch'), may hold values from -0.1875 to 0.1875
- w_out: bfloat16 [128, 4096, 1024], P('seq', 'batch'), may hold values from -0.09375 to 0.09375
- grad_out: bfloat16 [4, 32768, 1024], P('batch', 'seq'), may hold values from -6 to 6
Outputs:
- mixed: bfloat16 [4, 32768, 1024], P('batch', 'seq')
- grad_tokens: bfloat16 [4, 32768, 1024], P('batch', 'seq')
- grad_params: float32 [1024, 256], P(('batch', 'seq'))
The draws below stay inside these ranges and needn't reach their ends.
All inputs are finite; a program needn't handle non-finite values.
Results may differ from the reference program's by a relative error of at most 0.024.
Values may be sent and summed in bfloat16 or wider, within the bound.
No kernel may reach another device: no remote copies, remote signals or barrier semaphores. Data moves between devices by JAX's collectives and lax.ppermute only.
A program may use at most 64 MiB of HBM per device.

```python
import jax
import jax.numpy as jnp
from jax import lax

MODEL_WIDTH = 1024
MLP_DIM = 4096
EXPERTS = 128
TOTAL_SLOTS = 256
VIDEOS = 4
SEQLEN = 32768


def draw_tokens(key, part):
    key = jax.random.fold_in(key, 11)
    base_key_seed = jax.random.fold_in(key, 0)
    value_rows = jax.random.truncated_normal(base_key_seed, -6.0, 6.0, (VIDEOS, SEQLEN, MODEL_WIDTH), jnp.float32)
    return value_rows.astype(jnp.bfloat16)


def draw_slot_parameters(key, part):
    key = jax.random.fold_in(key, 23)
    base_key_seed = jax.random.fold_in(key, 0)
    value_rows = jax.random.truncated_normal(base_key_seed, -6.0, 6.0, (MODEL_WIDTH, TOTAL_SLOTS), jnp.float32) * 0.05
    return value_rows.astype(jnp.bfloat16)


def levels(stream_key, dims, pieces, low, high):
    level = 1.0
    for axis_at, shards_of in pieces:
        heights = jax.random.uniform(jax.random.fold_in(jax.random.fold_in(stream_key, 6), axis_at), (shards_of,), jnp.float32, low / len(pieces), high / len(pieces))
        level = level * jnp.repeat(jnp.exp(heights), dims[axis_at] // shards_of).reshape((-1,) + (1,) * (len(dims) - 1 - axis_at))
    return level


def centred(own_key, shape, width, reach, shards=(), held_as=jnp.bfloat16):
    values = width * jax.random.normal(own_key, shape, jnp.float32)
    if shards:
        values = values * levels(own_key, shape, shards, -0.22, 0.18)
    return jnp.clip(values, -reach, reach).astype(held_as)


def setup_inputs(seed: int = 0) -> dict:
    splits = jax.random.split(jax.random.key(seed), 6)
    return {
        "tokens": draw_tokens(jax.random.fold_in(splits[5], 71), 0),
        "slot_parameters": draw_slot_parameters(jax.random.fold_in(splits[5], 71), 0),
        "w_in": centred(splits[2], (EXPERTS, MODEL_WIDTH, MLP_DIM), MODEL_WIDTH ** -0.5, 0.1875, ((0, 64), (2, 4))),
        "w_out": centred(splits[3], (EXPERTS, MLP_DIM, MODEL_WIDTH), MLP_DIM ** -0.5, 0.09375, ((0, 64), (1, 4))),
        "grad_out": centred(splits[4], (VIDEOS, SEQLEN, MODEL_WIDTH), 1.0, 6.0, ((0, 4), (1, 64))),
    }


def gelu_exact(value_rows):
    return jax.nn.gelu(value_rows, approximate=False)

def to_expert_rows(slot_row_block, expert_list):
    video_batch, slot_number, width_size = slot_row_block.shape
    per_device = slot_number // expert_list
    return slot_row_block.reshape(video_batch, expert_list, per_device, width_size).transpose(1, 0, 2, 3).reshape(expert_list, video_batch * per_device, width_size)

def from_expert_rows(expert_rows, video_batch):
    expert_list, rows, width_size = expert_rows.shape
    per_device = rows // video_batch
    return expert_rows.reshape(expert_list, video_batch, per_device, width_size).transpose(1, 0, 2, 3).reshape(video_batch, expert_list * per_device, width_size)

def reference(tokens, slot_parameters, w_in, w_out, grad_out):
    video_batch = tokens.shape[0]
    expert_list = w_in.shape[0]
    logit_list, dexp_list, total_list, full_list = ([], [], [], [])
    for video in range(video_batch):
        source = tokens[video]
        logits = jnp.dot(source, slot_parameters, preferred_element_type=jnp.float32)
        peak = lax.optimization_barrier(jnp.max(logits, axis=0))
        dexp = jnp.exp(logits - peak).astype(jnp.bfloat16)
        total = lax.optimization_barrier(jnp.sum(dexp.astype(jnp.float32), axis=0))
        numer = jnp.dot(dexp.T, source, preferred_element_type=jnp.float32)
        logit_list.append(logits)
        dexp_list.append(dexp)
        total_list.append(total)
        full_list.append(numer / total[:, None])
    slot_full = jnp.stack(full_list)
    slot_in = slot_full.astype(jnp.bfloat16)
    rows_in = to_expert_rows(slot_in, expert_list)

    def expert_forward(operands):
        rows, first, second = operands
        pre = jnp.dot(rows, first, preferred_element_type=jnp.float32)
        act = gelu_exact(pre).astype(jnp.bfloat16)
        return (pre, jnp.dot(act, second, preferred_element_type=jnp.float32))
    pre_all, out_rows = lax.map(expert_forward, (rows_in, w_in, w_out))
    slot_out = from_expert_rows(out_rows, video_batch).astype(jnp.bfloat16)
    mixed_list, comb_list, dlog_list, dslot_list = ([], [], [], [])
    for video in range(video_batch):
        combine = jax.nn.softmax(logit_list[video], axis=1)
        combine_b = combine.astype(jnp.bfloat16)
        mixed_list.append(jnp.dot(combine_b, slot_out[video], preferred_element_type=jnp.float32).astype(jnp.bfloat16))
        cotan = grad_out[video]
        dcomb = jnp.dot(cotan, slot_out[video].T, preferred_element_type=jnp.float32)
        dlog_list.append(combine * (dcomb - lax.optimization_barrier(jnp.sum(combine * dcomb, axis=1, keepdims=True))))
        dslot_list.append(jnp.dot(combine_b.T, cotan, preferred_element_type=jnp.float32))
    dslot_out = jnp.stack(dslot_list).astype(jnp.bfloat16)
    rows_grad = to_expert_rows(dslot_out, expert_list)

    def expert_backward(operands):
        rows, pre, first, second = operands
        dact = jnp.dot(rows, second.T, preferred_element_type=jnp.float32)
        unused, pullback = jax.vjp(gelu_exact, pre)
        dpre = pullback(dact)[0].astype(jnp.bfloat16)
        return jnp.dot(dpre, first.T, preferred_element_type=jnp.float32)
    back_rows = lax.map(expert_backward, (rows_grad, pre_all, w_in, w_out))
    dslot_in = from_expert_rows(back_rows, video_batch)
    grad_list = []
    grad_params = jnp.zeros(slot_parameters.shape, jnp.float32)
    for video in range(video_batch):
        source = tokens[video]
        scaled = (dslot_in[video] / total_list[video][:, None]).astype(jnp.bfloat16)
        inner = jnp.dot(source, scaled.T, preferred_element_type=jnp.float32)
        shift = lax.optimization_barrier(jnp.sum(slot_full[video] * scaled.astype(jnp.float32), axis=1))
        dlog = dlog_list[video] + dexp_list[video].astype(jnp.float32) * (inner - shift)
        dlog_b = dlog.astype(jnp.bfloat16)
        grad_in = jnp.dot(dlog_b, slot_parameters.T, preferred_element_type=jnp.float32)
        grad_in = grad_in + jnp.dot(dexp_list[video], scaled, preferred_element_type=jnp.float32)
        grad_list.append(grad_in.astype(jnp.bfloat16))
        grad_params = grad_params + jnp.dot(source.T, dlog_b, preferred_element_type=jnp.float32)
    return (jnp.stack(mixed_list), jnp.stack(grad_list), grad_params)
```

```python
import jax
import jax.numpy as jnp
from jax import lax
from jax.experimental import pallas as pl
from jax.experimental.pallas import tpu as pltpu
from jax.sharding import Mesh, PartitionSpec as P

BF = jnp.bfloat16
F32 = jnp.float32
AXES = ("x", "z", "y", "c")
ZY = ("z", "y")
STAT = 128
PARAMS = pltpu.CompilerParams(vmem_limit_bytes=40 * 1024 * 1024)


def dot(a, b, contract=((1,), (0,))):
    return lax.dot_general(a, b, (contract, ((), ())), preferred_element_type=F32)


def iota(shape, dim):
    return lax.broadcasted_iota(jnp.int32, shape, dim)


def call(body, outs, *args, flops=0, scratch=(), params=PARAMS):
    nbytes = sum(a.size * a.dtype.itemsize for a in args)
    nbytes += sum(o.size * o.dtype.itemsize for o in outs)
    return pl.pallas_call(
        body,
        out_shape=outs,
        in_specs=[pl.BlockSpec(memory_space=pltpu.VMEM)] * len(args),
        out_specs=[pl.BlockSpec(memory_space=pltpu.VMEM)] * len(outs),
        scratch_shapes=list(scratch),
        compiler_params=params,
        cost_estimate=pl.CostEstimate(flops=flops, bytes_accessed=nbytes, transcendentals=0),
    )(*args)


def split(value):
    high = value.astype(BF).astype(F32)
    return high, (value - high).astype(BF).astype(F32)


def stats(lane, first, second, third):
    return jnp.where(lane == 0, first, jnp.where(lane == 1, second, jnp.where(lane == 2, third, 0.0)))


def softmax_rows(logits):
    e = jnp.exp(logits - jnp.max(logits, axis=1, keepdims=True))
    return e / jnp.sum(e, axis=1, keepdims=True)


def reduce_tokens(tok_ref, cot_ref, par_ref, keep_ref, send_ref, logit_ref):
    core = lax.axis_index("c")
    tok = tok_ref[...]
    logits = dot(tok, par_ref[...])
    logit_ref[...] = logits
    n = logits.shape[1]
    refpoint = jnp.max(logits, axis=0, keepdims=True).astype(BF).astype(F32)
    dexp = jnp.exp(logits - refpoint).astype(BF)
    comb = softmax_rows(logits).astype(BF)
    numer = dot(dexp, tok, ((0,), (0,)))
    dslot = dot(comb, cot_ref[...], ((0,), (0,)))
    total = dot(dexp, jnp.ones((tok.shape[0], STAT), BF), ((0,), (0,)))
    diag = jnp.where(iota((n, n), 0) == iota((n, n), 1), refpoint, 0.0).astype(BF)
    point = dot(diag, jnp.ones((n, STAT), BF))
    high, low = split(total)
    side = stats(iota((n, STAT), 1), point, high, low).astype(BF)
    upper = jnp.concatenate([numer.astype(BF), side], axis=1)
    lower = jnp.concatenate([dslot.astype(BF), jnp.zeros((n, STAT), BF)], axis=1)
    rows = jnp.concatenate([upper, lower], axis=0)
    row, col = iota((n, 2 * n), 0), iota((n, 2 * n), 1)
    for ref, c in ((keep_ref, core), (send_ref, 1 - core)):
        want = (row // 8) * 8 + c * 4 + row % 4 + ((row // 4) % 2) * n
        ref[...] = dot((col == want).astype(BF), rows).astype(BF)


def merge_cores(a_ref, b_ref, out_ref):
    a, b = a_ref[...].astype(F32), b_ref[...].astype(F32)
    width = a.shape[1] - STAT
    ma, mb = a[:, width:width + 1], b[:, width:width + 1]
    top = jnp.maximum(ma, mb)
    sa, sb = jnp.exp(ma - top), jnp.exp(mb - top)
    out_ref[:, :width] = (sa * a[:, :width] + sb * b[:, :width]).astype(BF)
    ta = a[:, width + 1:width + 2] + a[:, width + 2:width + 3]
    tb = b[:, width + 1:width + 2] + b[:, width + 2:width + 3]
    high, low = split(sa * ta + sb * tb)
    out_ref[:, width:] = stats(iota((a.shape[0], STAT), 1), top, high, low).astype(BF)


def merge_shards(in_ref, pay_ref, full_ref, side_ref):
    value = in_ref[...].astype(F32)
    width = value.shape[2] - STAT
    point = value[:, :, width:width + 1]
    top = jnp.max(point, axis=0)
    scale = jnp.exp(point - top[None])
    total = jnp.sum(scale * (value[:, :, width + 1:width + 2] + value[:, :, width + 2:width + 3]), axis=0)
    acc = jnp.sum(scale * value[:, :, :width], axis=0)
    slots = acc.shape[0] // 2
    first = iota((2 * slots, 1), 0) < slots
    full = acc / jnp.where(first, total, 1.0)
    full_ref[...] = full
    both = jnp.concatenate([total[:slots], total[:slots]], axis=0)
    side_ref[...] = jnp.where(iota((2 * slots, STAT), 1) == 0, top, both)
    pay_ref[...] = jnp.broadcast_to(full.astype(BF)[None], pay_ref.shape)


def gelu_parts(u):
    cdf = 0.5 * (1.0 + lax.erf(u * 0.7071067811865476))
    pdf = 0.3989422804014327 * jnp.exp(-0.5 * u * u)
    return u * cdf, cdf + u * pdf


def experts(x_ref, win_ref, wout_ref, out_ref, f_ref, g_ref, o_acc, d_acc):
    e, h = pl.program_id(0), pl.program_id(1)
    rows = f_ref.shape[0]

    @pl.when((e == 0) & (h == 0))
    def _():
        row, col = iota((rows, 2 * rows), 0), iota((rows, 2 * rows), 1)
        want = (row // 4) * 8 + row % 4
        x = x_ref[...]
        f_ref[...] = dot((col == want).astype(BF), x).astype(BF)
        g_ref[...] = dot((col == want + 4).astype(BF), x).astype(BF)
        o_acc[...] = jnp.zeros_like(o_acc)
        d_acc[...] = jnp.zeros_like(d_acc)

    w1, w2 = win_ref[0], wout_ref[0]
    mine = (iota((rows, 1), 0) % 4) // 2 == e
    pre = dot(f_ref[...], w1)
    gelu, slope = gelu_parts(pre)
    act = jnp.where(mine, gelu, 0.0).astype(BF)
    o_acc[...] += dot(act, w2)
    dact = dot(g_ref[...], w2, ((1,), (1,)))
    dpre = jnp.where(mine, dact * slope, 0.0).astype(BF)
    d_acc[...] += dot(dpre, w1, ((1,), (1,)))

    @pl.when((e == pl.num_programs(0) - 1) & (h == pl.num_programs(1) - 1))
    def _():
        for v in range(rows // 4):
            out_ref[v, 0:4, :] = o_acc[4 * v:4 * v + 4, :]
            out_ref[v, 4:8, :] = d_acc[4 * v:4 * v + 4, :]


def finish_slots(in_ref, full_ref, side_ref, out_ref):
    value = jnp.sum(in_ref[...], axis=0)
    width = value.shape[1]
    slots = value.shape[0] // 2
    first = iota((2 * slots, 1), 0) < slots
    side = side_ref[...]
    body = jnp.where(first, value, value / side[:, 1:2]).astype(BF)
    wide = body.astype(F32)
    shift = jnp.sum(full_ref[:slots, :] * wide[slots:, :], axis=1, keepdims=True)
    shift = jnp.concatenate([shift, shift], axis=0)
    high, low = split(shift)
    st = stats(iota((2 * slots, STAT), 1), side[:, 0:1], high, low).astype(BF)
    block = jnp.concatenate([body, st], axis=1)
    out_ref[...] = jnp.broadcast_to(block[None], out_ref.shape)


def token_grads(logit_ref, tok_ref, cot_ref, own_ref, oth_ref,
                keep_ref, send_ref, dlog_ref, dexp_ref, comb_ref, so_ref, sc_ref):
    core = lax.axis_index("c")
    logits, tok = logit_ref[...], tok_ref[...]
    n = logits.shape[1]
    width = tok.shape[1]
    rows = jnp.concatenate([own_ref[...], oth_ref[...]], axis=0)
    slot, col = iota((n, 2 * n), 0), iota((n, 2 * n), 1)
    want = (slot // 8) * 8 + slot % 4 + jnp.where((slot // 4) % 2 == core, 0, n)
    first = dot((col == want).astype(BF), rows)
    second = dot((col == want + 4).astype(BF), rows[:, :width])
    slot_out, scaled = first[:, :width].astype(BF), second.astype(BF)
    so_ref[...] = slot_out
    sc_ref[...] = scaled
    side = first[:, width:].T
    point, shift = side[0:1, :], side[1:2, :] + side[2:3, :]
    comb = softmax_rows(logits)
    comb_ref[...] = comb.astype(BF)
    dexp = jnp.exp(logits - point).astype(BF)
    dexp_ref[...] = dexp
    dcomb = dot(cot_ref[...], slot_out, ((1,), (1,)))
    inner = dot(tok, scaled, ((1,), (1,)))
    dlog = comb * (dcomb - jnp.sum(comb * dcomb, axis=1, keepdims=True))
    dlog = (dlog + dexp.astype(F32) * (inner - shift)).astype(BF)
    dlog_ref[...] = dlog
    gp = dot(tok, dlog, ((0,), (0,))).reshape(width // 8, 8, n)
    low, high = gp[:, 0:4, :], gp[:, 4:8, :]
    keep_ref[...] = jnp.where(core == 0, low, high).astype(BF)
    send_ref[...] = jnp.where(core == 0, high, low).astype(BF)


def token_outputs(comb_ref, so_ref, dlog_ref, par_ref, dexp_ref, sc_ref, mixed_ref, grad_ref):
    mixed_ref[...] = dot(comb_ref[...], so_ref[...]).astype(BF)
    grad = dot(dlog_ref[...], par_ref[...], ((1,), (1,)))
    grad_ref[...] = (grad + dot(dexp_ref[...], sc_ref[...])).astype(BF)


def on_device(tokens, slot_parameters, w_in, w_out, grad_out):
    shape = jax.ShapeDtypeStruct
    tok, cot = tokens[0], grad_out[0]
    count, width = tok.shape
    n = slot_parameters.shape[1]
    videos = lax.axis_size("x")
    owners = lax.axis_size("z") * lax.axis_size("y")
    wide = width + STAT
    unit = 2 * count * width * n
    swap = [(0, 1), (1, 0)]

    keep, send, logits = call(
        reduce_tokens,
        [shape((n, wide), BF), shape((n, wide), BF), shape((count, n), F32)],
        tok, cot, slot_parameters, flops=5 * unit,
    )
    other = lax.ppermute(send, "c", swap)
    (merged,) = call(merge_cores, [shape((n, wide), BF)], keep, other)
    shards = lax.all_to_all(merged.reshape(owners, 8, wide), ZY, 0, 0, tiled=True)
    pay, full, side = call(
        merge_shards,
        [shape((videos, 8, width), BF), shape((8, width), F32), shape((8, STAT), F32)],
        shards,
    )
    stacked = lax.all_to_all(pay, "x", 0, 0, tiled=True)

    hidden = w_in.shape[2]
    chunk = 256
    rows = 4 * videos
    partial = pl.pallas_call(
        experts,
        grid=(w_in.shape[0], hidden // chunk),
        in_specs=[
            pl.BlockSpec((2 * rows, width), lambda e, h: (0, 0)),
            pl.BlockSpec((1, width, chunk), lambda e, h: (e, 0, h)),
            pl.BlockSpec((1, chunk, width), lambda e, h: (e, h, 0)),
        ],
        out_specs=pl.BlockSpec((videos, 8, width), lambda e, h: (0, 0, 0)),
        out_shape=shape((videos, 8, width), F32),
        scratch_shapes=[
            pltpu.VMEM((rows, width), BF), pltpu.VMEM((rows, width), BF),
            pltpu.VMEM((rows, width), F32), pltpu.VMEM((rows, width), F32),
        ],
        compiler_params=PARAMS,
        cost_estimate=pl.CostEstimate(flops=8 * rows * w_in.size, bytes_accessed=4 * w_in.size, transcendentals=0),
    )(stacked.reshape(2 * rows, width), w_in, w_out)
    parts = lax.all_to_all(partial, "x", 0, 0, tiled=True)
    (block,) = call(finish_slots, [shape((owners, 8, wide), BF)], parts, full, side)
    mine = lax.all_to_all(block, ZY, 0, 0, tiled=True).reshape(n, wide)
    theirs = lax.ppermute(mine, "c", swap)

    gp_keep, gp_send, dlog, dexp, comb, slot_out, scaled = call(
        token_grads,
        [shape((width // 8, 4, n), BF), shape((width // 8, 4, n), BF),
         shape((count, n), BF), shape((count, n), BF), shape((count, n), BF),
         shape((n, width), BF), shape((n, width), BF)],
        logits, tok, cot, mine, theirs, flops=5 * unit,
    )
    gp_other = lax.ppermute(gp_send, "c", swap)
    mixed, grad_tokens = call(
        token_outputs,
        [shape((count, width), BF), shape((count, width), BF)],
        comb, slot_out, dlog, slot_parameters, dexp, scaled, flops=3 * unit,
    )
    half = (gp_keep.astype(F32) + gp_other.astype(F32)).astype(BF)
    pieces = lax.all_to_all(half, ("x", "z", "y"), 0, 0, tiled=True)
    grad_params = jnp.sum(pieces.astype(F32), axis=0)
    return mixed[None], grad_tokens[None], grad_params


def solution(mesh):
    sizes = dict(mesh.shape)
    grid = Mesh(mesh.devices.reshape(sizes["batch"], sizes["seq"] // 8, 4, 2), AXES)
    seq = ("z", "y", "c")
    placed = (
        P("x", seq, None),
        P(),
        P(seq, None, "x"),
        P(seq, "x", None),
        P("x", seq, None),
    )
    return jax.shard_map(
        on_device,
        mesh=grid,
        in_specs=placed,
        out_specs=(P("x", seq, None), P("x", seq, None), P(AXES, None)),
        check_vma=False,
    )
```

```python
import jax
import jax.numpy as jnp
from jax import lax
from jax.experimental import pallas as pl
from jax.experimental.pallas import tpu as pltpu
from jax.sharding import Mesh, PartitionSpec as P

BF = jnp.bfloat16
F32 = jnp.float32
AXES = ("x", "z", "y", "c")
ZY = ("z", "y")
PARTS = 4
STAT = 128
PARAMS = pltpu.CompilerParams(vmem_limit_bytes=24 * 1024 * 1024)


def dot(a, b, contract=((1,), (0,))):
    return lax.dot_general(a, b, (contract, ((), ())), preferred_element_type=F32)


def iota(shape, dim):
    return lax.broadcasted_iota(jnp.int32, shape, dim)


def call(body, outs, *args, flops=0, scratch=(), params=PARAMS):
    nbytes = sum(a.size * a.dtype.itemsize for a in args)
    nbytes += sum(o.size * o.dtype.itemsize for o in outs)
    return pl.pallas_call(
        body,
        out_shape=outs,
        in_specs=[pl.BlockSpec(memory_space=pltpu.VMEM)] * len(args),
        out_specs=[pl.BlockSpec(memory_space=pltpu.VMEM)] * len(outs),
        scratch_shapes=list(scratch),
        compiler_params=params,
        cost_estimate=pl.CostEstimate(flops=flops, bytes_accessed=nbytes, transcendentals=0),
    )(*args)


def split(value):
    high = value.astype(BF).astype(F32)
    return high, (value - high).astype(BF).astype(F32)


def stats(lane, first, second, third):
    return jnp.where(lane == 0, first, jnp.where(lane == 1, second, jnp.where(lane == 2, third, 0.0)))


def softmax_rows(logits):
    e = jnp.exp(logits - jnp.max(logits, axis=1, keepdims=True))
    return e / jnp.sum(e, axis=1, keepdims=True)


def swap_halves(value):
    return pltpu.roll(value, 4, 1)


def reduce_tokens(tok_hbm, cot_hbm, par_hbm, keep_ref, send_ref, logit_ref,
                  tok_ref, cot_ref, par_ref, comb_ref, sems):
    core = lax.axis_index("c")
    count, width = tok_ref.shape
    n = par_ref.shape[1]
    part = count // PARTS
    copies = [pltpu.make_async_copy(par_hbm, par_ref, sems.at[0])]
    for i in range(PARTS):
        rows = pl.ds(i * part, part)
        copies.append(pltpu.make_async_copy(tok_hbm.at[rows], tok_ref.at[rows], sems.at[1 + i]))
    copies.append(pltpu.make_async_copy(cot_hbm, cot_ref, sems.at[1 + PARTS]))
    for copy in copies:
        copy.start()
    copies[0].wait()
    par = par_ref[...]
    peak = None
    for i in range(PARTS):
        rows = pl.ds(i * part, part)
        copies[1 + i].wait()
        piece = dot(tok_ref[rows, :], par)
        logit_ref[rows, :] = piece
        comb_ref[rows, :] = softmax_rows(piece).astype(BF)
        high = jnp.max(piece, axis=0, keepdims=True)
        peak = high if peak is None else jnp.maximum(peak, high)
    refpoint = peak.astype(BF).astype(F32)
    dexp = jnp.exp(logit_ref[...] - refpoint).astype(BF)
    numer = dot(dexp, tok_ref[...], ((0,), (0,))).reshape(n // 8, 8, width)
    total = dot(dexp, jnp.ones((count, STAT), BF), ((0,), (0,)))
    diag = jnp.where(iota((n, n), 0) == iota((n, n), 1), refpoint, 0.0).astype(BF)
    point = dot(diag, jnp.ones((n, STAT), BF))
    high, low = split(total)
    side = stats(iota((n, STAT), 1), point, high, low).reshape(n // 8, 8, STAT)
    copies[1 + PARTS].wait()
    dslot = dot(comb_ref[...], cot_ref[...], ((0,), (0,))).reshape(n // 8, 8, width)
    upper = iota((1, 8, 1), 1) < 4
    zero = core == 0
    even = jnp.where(upper, numer, swap_halves(dslot)).astype(BF)
    odd = jnp.where(upper, swap_halves(numer), dslot).astype(BF)
    even_side = jnp.where(upper, side, 0.0).astype(BF)
    odd_side = jnp.where(upper, swap_halves(side), 0.0).astype(BF)
    keep_ref[:, :, :width] = jnp.where(zero, even, odd)
    send_ref[:, :, :width] = jnp.where(zero, odd, even)
    keep_ref[:, :, width:] = jnp.where(zero, even_side, odd_side)
    send_ref[:, :, width:] = jnp.where(zero, odd_side, even_side)


def merge_cores(a_ref, b_ref, out_ref):
    a, b = a_ref[...].astype(F32), b_ref[...].astype(F32)
    width = a.shape[2] - STAT
    ma, mb = a[:, :, width:width + 1], b[:, :, width:width + 1]
    top = jnp.maximum(ma, mb)
    sa, sb = jnp.exp(ma - top), jnp.exp(mb - top)
    out_ref[:, :, :width] = (sa * a[:, :, :width] + sb * b[:, :, :width]).astype(BF)
    ta = a[:, :, width + 1:width + 2] + a[:, :, width + 2:width + 3]
    tb = b[:, :, width + 1:width + 2] + b[:, :, width + 2:width + 3]
    high, low = split(sa * ta + sb * tb)
    lane = iota((a.shape[0], 8, STAT), 2)
    out_ref[:, :, width:] = stats(lane, top, high, low).astype(BF)


def merge_shards(in_ref, pay_ref, full_ref, side_ref):
    value = in_ref[...].astype(F32)
    width = value.shape[2] - STAT
    point = value[:, :, width:width + 1]
    top = jnp.max(point, axis=0)
    scale = jnp.exp(point - top[None])
    total = jnp.sum(scale * (value[:, :, width + 1:width + 2] + value[:, :, width + 2:width + 3]), axis=0)
    acc = jnp.sum(scale * value[:, :, :width], axis=0)
    slots = acc.shape[0] // 2
    first = iota((2 * slots, 1), 0) < slots
    full = acc / jnp.where(first, total, 1.0)
    full_ref[...] = full
    both = jnp.concatenate([total[:slots], total[:slots]], axis=0)
    side_ref[...] = jnp.where(iota((2 * slots, STAT), 1) == 0, top, both)
    pay_ref[...] = full.astype(BF)


def gelu_parts(u):
    cdf = 0.5 * (1.0 + lax.erf(u * 0.7071067811865476))
    pdf = 0.3989422804014327 * jnp.exp(-0.5 * u * u)
    return u * cdf, cdf + u * pdf


def experts(own_ref, a_ref, b_ref, c_ref, win_ref, wout_ref, *out_refs):
    blocks = [r[...].astype(F32) for r in (own_ref, a_ref, b_ref, c_ref)]
    fwd = jnp.concatenate([x[:4] for x in blocks], axis=0).astype(BF)
    bwd = jnp.concatenate([x[4:] for x in blocks], axis=0).astype(BF)
    rows = fwd.shape[0]
    out, back = 0.0, 0.0
    for e in range(win_ref.shape[0]):
        mine = (iota((rows, 1), 0) % 4) // 2 == e
        w1, w2 = win_ref[e], wout_ref[e]
        gelu, slope = gelu_parts(dot(fwd, w1))
        out += dot(jnp.where(mine, gelu, 0.0).astype(BF), w2)
        dact = dot(bwd, w2, ((1,), (1,)))
        back += dot(jnp.where(mine, dact * slope, 0.0).astype(BF), w1, ((1,), (1,)))
    for v, ref in enumerate(out_refs):
        ref[...] = jnp.concatenate([out[4 * v:4 * v + 4], back[4 * v:4 * v + 4]], axis=0)


def finish_slots(own_ref, a_ref, b_ref, c_ref, full_ref, side_ref, out_ref):
    value = (own_ref[...] + a_ref[...]) + (b_ref[...] + c_ref[...])
    width = value.shape[1]
    slots = value.shape[0] // 2
    first = iota((2 * slots, 1), 0) < slots
    side = side_ref[...]
    body = jnp.where(first, value, value / side[:, 1:2]).astype(BF)
    wide = body.astype(F32)
    shift = jnp.sum(full_ref[:slots, :] * wide[slots:, :], axis=1, keepdims=True)
    shift = jnp.concatenate([shift, shift], axis=0)
    high, low = split(shift)
    st = stats(iota((2 * slots, STAT), 1), side[:, 0:1], high, low).astype(BF)
    block = jnp.concatenate([body, st], axis=1)
    out_ref[...] = jnp.broadcast_to(block[None], out_ref.shape)


def token_grads(logit_ref, tok_ref, cot_ref, own_ref, oth_ref,
                keep_ref, send_ref, dlog_ref, dexp_ref, comb_ref, so_ref, sc_ref):
    core = lax.axis_index("c")
    logits, tok = logit_ref[...], tok_ref[...]
    n = logits.shape[1]
    width = tok.shape[1]
    zero = core == 0
    upper = iota((1, 8, 1), 1) < 4
    own, oth = own_ref[...].astype(F32), oth_ref[...].astype(F32)
    even, odd = jnp.where(zero, own, oth), jnp.where(zero, oth, own)
    first = jnp.where(upper, even, swap_halves(odd)).reshape(n, width + STAT)
    second = jnp.where(upper, swap_halves(even), odd).reshape(n, width + STAT)
    slot_out, scaled = first[:, :width].astype(BF), second[:, :width].astype(BF)
    so_ref[...] = slot_out
    sc_ref[...] = scaled
    side = first[:, width:].T
    point, shift = side[0:1, :], side[1:2, :] + side[2:3, :]
    comb = softmax_rows(logits)
    comb_ref[...] = comb.astype(BF)
    dexp = jnp.exp(logits - point).astype(BF)
    dexp_ref[...] = dexp
    dcomb = dot(cot_ref[...], slot_out, ((1,), (1,)))
    inner = dot(tok, scaled, ((1,), (1,)))
    dlog = comb * (dcomb - jnp.sum(comb * dcomb, axis=1, keepdims=True))
    dlog = (dlog + dexp.astype(F32) * (inner - shift)).astype(BF)
    dlog_ref[...] = dlog
    gp = dot(tok, dlog, ((0,), (0,))).reshape(width // 8, 8, n)
    left, right = gp[:, :, :n // 2], gp[:, :, n // 2:]
    even = jnp.where(upper, left, swap_halves(right)).astype(BF)
    odd = jnp.where(upper, swap_halves(left), right).astype(BF)
    keep_ref[...] = jnp.where(zero, even, odd)
    send_ref[...] = jnp.where(zero, odd, even)


def token_outputs(comb_ref, so_ref, dlog_ref, par_ref, dexp_ref, sc_ref, mixed_ref, grad_ref):
    mixed_ref[...] = dot(comb_ref[...], so_ref[...]).astype(BF)
    grad = dot(dlog_ref[...], par_ref[...], ((1,), (1,)))
    grad_ref[...] = (grad + dot(dexp_ref[...], sc_ref[...])).astype(BF)


def add_halves(a_ref, b_ref, out_ref):
    out_ref[...] = (a_ref[...].astype(F32) + b_ref[...].astype(F32)).astype(BF)


def sum_pieces(in_ref, out_ref):
    total = jnp.sum(in_ref[...].astype(F32), axis=0)
    half = total.shape[1]
    out_ref[:, :half] = total[:4]
    out_ref[:, half:] = total[4:]


def shifted(value, step, size):
    return lax.ppermute(value, "x", [(i, (i + step) % size) for i in range(size)])


def on_device(tokens, slot_parameters, w_in, w_out, grad_out):
    shape = jax.ShapeDtypeStruct
    tok, cot = tokens[0], grad_out[0]
    count, width = tok.shape
    n = slot_parameters.shape[1]
    videos = lax.axis_size("x")
    owners = lax.axis_size("z") * lax.axis_size("y")
    wide = width + STAT
    unit = 2 * count * width * n
    swap = [(0, 1), (1, 0)]

    vmem = pl.BlockSpec(memory_space=pltpu.VMEM)
    keep, send, logits = pl.pallas_call(
        reduce_tokens,
        out_shape=[shape((owners, 8, wide), BF), shape((owners, 8, wide), BF), shape((count, n), F32)],
        in_specs=[pl.BlockSpec(memory_space=pltpu.HBM)] * 3,
        out_specs=[vmem] * 3,
        scratch_shapes=[
            pltpu.VMEM((count, width), BF), pltpu.VMEM((count, width), BF),
            pltpu.VMEM((width, n), BF), pltpu.VMEM((count, n), BF),
            pltpu.SemaphoreType.DMA((PARTS + 2,)),
        ],
        compiler_params=PARAMS,
        cost_estimate=pl.CostEstimate(flops=4 * unit, bytes_accessed=4 << 20, transcendentals=0),
    )(*[pltpu.with_memory_space_constraint(a, pltpu.HBM) for a in (tok, cot, slot_parameters)])
    other = lax.ppermute(send, "c", swap)
    (merged,) = call(merge_cores, [shape((owners, 8, wide), BF)], keep, other, flops=40 * unit)
    shards = lax.all_to_all(merged, ZY, 0, 0, tiled=True)
    pay, full, side = call(
        merge_shards,
        [shape((8, width), BF), shape((8, width), F32), shape((8, STAT), F32)],
        shards,
    )
    behind = [shifted(pay, k, videos) for k in range(1, videos)]
    partial = call(
        experts, [shape((8, width), F32)] * videos, pay, *behind, w_in, w_out,
        flops=32 * videos * w_in.size,
    )
    parts = [shifted(partial[k], -k, videos) for k in range(1, videos)]
    (block,) = call(finish_slots, [shape((owners, 8, wide), BF)], partial[0], *parts, full, side)
    mine = lax.all_to_all(block, ZY, 0, 0, tiled=True)
    theirs = lax.ppermute(mine, "c", swap)

    gp_keep, gp_send, dlog, dexp, comb, slot_out, scaled = call(
        token_grads,
        [shape((width // 8, 8, n // 2), BF), shape((width // 8, 8, n // 2), BF),
         shape((count, n), BF), shape((count, n), BF), shape((count, n), BF),
         shape((n, width), BF), shape((n, width), BF)],
        logits, tok, cot, mine, theirs, flops=5 * unit,
    )
    gp_other = lax.ppermute(gp_send, "c", swap)
    mixed, grad_tokens = call(
        token_outputs,
        [shape((count, width), BF), shape((count, width), BF)],
        comb, slot_out, dlog, slot_parameters, dexp, scaled, flops=3 * unit,
    )
    (half,) = call(add_halves, [shape(gp_keep.shape, BF)], gp_keep, gp_other)
    pieces = lax.all_to_all(half, ("x", "z", "y"), 0, 0, tiled=True)
    (grad_params,) = call(sum_pieces, [shape((4, n), F32)], pieces)
    return mixed[None], grad_tokens[None], grad_params


def solution(mesh):
    sizes = dict(mesh.shape)
    grid = Mesh(mesh.devices.reshape(sizes["batch"], sizes["seq"] // 8, 4, 2), AXES)
    seq = ("z", "y", "c")
    placed = (
        P("x", seq, None),
        P(),
        P(seq, None, "x"),
        P(seq, "x", None),
        P("x", seq, None),
    )
    return jax.shard_map(
        on_device,
        mesh=grid,
        in_specs=placed,
        out_specs=(P("x", seq, None), P("x", seq, None), P(AXES, None)),
        check_vma=False,
    )
```

```python
import math

import jax
import jax.numpy as jnp
from jax import lax
from jax.experimental import pallas as pl
from jax.experimental.pallas import tpu as pltpu
from jax.sharding import Mesh, PartitionSpec as P

BF = jnp.bfloat16
F32 = jnp.float32
AXES = ("x", "z", "y", "c")
ZY = ("z", "y")
PARTS = 2
STAT = 128
PARAMS = pltpu.CompilerParams(vmem_limit_bytes=24 * 1024 * 1024)


def dot(a, b, contract=((1,), (0,))):
    return lax.dot_general(a, b, (contract, ((), ())), preferred_element_type=F32)


def iota(shape, dim):
    return lax.broadcasted_iota(jnp.int32, shape, dim)


def call(body, outs, *args, flops=0, scratch=(), params=PARAMS):
    nbytes = sum(a.size * a.dtype.itemsize for a in args)
    nbytes += sum(math.prod(o.shape) * 4 for o in outs)
    return pl.pallas_call(
        body,
        out_shape=outs,
        in_specs=[pl.BlockSpec(memory_space=pltpu.VMEM)] * len(args),
        out_specs=[pl.BlockSpec(memory_space=pltpu.VMEM)] * len(outs),
        scratch_shapes=list(scratch),
        compiler_params=params,
        cost_estimate=pl.CostEstimate(flops=flops, bytes_accessed=nbytes, transcendentals=0),
    )(*args)


def split(value):
    high = value.astype(BF).astype(F32)
    return high, (value - high).astype(BF).astype(F32)


def stats(lane, first, second, third):
    return jnp.where(lane == 0, first, jnp.where(lane == 1, second, jnp.where(lane == 2, third, 0.0)))


def softmax_rows(logits):
    e = jnp.exp(logits - jnp.max(logits, axis=1, keepdims=True))
    return e / jnp.sum(e, axis=1, keepdims=True)


def swap_halves(value):
    return pltpu.roll(value, 4, 1)


def reduce_tokens(tok_hbm, cot_hbm, par_hbm, keep_ref, send_ref, logit_ref,
                  tok_ref, cot_ref, par_ref, comb_ref, sems):
    core = lax.axis_index("c")
    count, width = tok_ref.shape
    n = par_ref.shape[1]
    part = count // PARTS
    copies = [pltpu.make_async_copy(par_hbm, par_ref, sems.at[0])]
    for i in range(PARTS):
        rows = pl.ds(i * part, part)
        copies.append(pltpu.make_async_copy(tok_hbm.at[rows], tok_ref.at[rows], sems.at[1 + i]))
    copies.append(pltpu.make_async_copy(cot_hbm, cot_ref, sems.at[1 + PARTS]))
    for copy in copies:
        copy.start()
    copies[0].wait()
    par = par_ref[...]
    peak = None
    for i in range(PARTS):
        rows = pl.ds(i * part, part)
        copies[1 + i].wait()
        piece = dot(tok_ref[rows, :], par)
        logit_ref[rows, :] = piece
        comb_ref[rows, :] = softmax_rows(piece).astype(BF)
        high = jnp.max(piece, axis=0, keepdims=True)
        peak = high if peak is None else jnp.maximum(peak, high)
    refpoint = peak.astype(BF).astype(F32)
    dexp = jnp.exp(logit_ref[...] - refpoint).astype(BF)
    numer = dot(dexp, tok_ref[...], ((0,), (0,))).reshape(n // 8, 8, width)
    total = dot(dexp, jnp.ones((count, STAT), BF), ((0,), (0,)))
    diag = jnp.where(iota((n, n), 0) == iota((n, n), 1), refpoint, 0.0).astype(BF)
    point = dot(diag, jnp.ones((n, STAT), BF))
    high, low = split(total)
    side = stats(iota((n, STAT), 1), point, high, low).reshape(n // 8, 8, STAT)
    copies[1 + PARTS].wait()
    dslot = dot(comb_ref[...], cot_ref[...], ((0,), (0,))).reshape(n // 8, 8, width)
    upper = iota((1, 8, 1), 1) < 4
    zero = core == 0
    even = jnp.where(upper, numer, swap_halves(dslot)).astype(BF)
    odd = jnp.where(upper, swap_halves(numer), dslot).astype(BF)
    even_side = jnp.where(upper, side, 0.0).astype(BF)
    odd_side = jnp.where(upper, swap_halves(side), 0.0).astype(BF)
    even = jnp.concatenate([even, even_side], axis=2)
    odd = jnp.concatenate([odd, odd_side], axis=2)
    for ref, value in ((keep_ref, jnp.where(zero, even, odd)), (send_ref, jnp.where(zero, odd, even))):
        value = value.reshape(n // 8 // ref.shape[0], *ref.shape[:1], 8, width + STAT)
        for y in range(ref.shape[0]):
            ref[y] = value[:, y]


def merge(parts):
    width = parts[0].shape[-1] - STAT
    points = [p[..., width:width + 1] for p in parts]
    top = points[0]
    for point in points[1:]:
        top = jnp.maximum(top, point)
    body, total = 0.0, 0.0
    for part, point in zip(parts, points):
        scale = jnp.exp(point - top)
        body += scale * part[..., :width]
        total += scale * (part[..., width + 1:width + 2] + part[..., width + 2:width + 3])
    return body, top, total


def store_merged(parts, out_ref):
    body, top, total = merge(parts)
    width = body.shape[-1]
    high, low = split(total)
    out_ref[..., :width] = body.astype(BF)
    lane = iota(body.shape[:-1] + (STAT,), body.ndim - 1)
    out_ref[..., width:] = stats(lane, top, high, low).astype(BF)


def merge_cores(a_ref, b_ref, out_ref):
    store_merged([a_ref[...].astype(F32), b_ref[...].astype(F32)], out_ref)


def merge_columns(in_ref, out_ref):
    store_merged([in_ref[i].astype(F32) for i in range(in_ref.shape[0])], out_ref)


def merge_shards(in_ref, pay_ref, full_ref, side_ref):
    acc, top, total = merge([in_ref[i].astype(F32) for i in range(in_ref.shape[0])])
    slots = acc.shape[0] // 2
    first = iota((2 * slots, 1), 0) < slots
    full = acc / jnp.where(first, total, 1.0)
    full_ref[...] = full
    both = jnp.concatenate([total[:slots], total[:slots]], axis=0)
    side_ref[...] = jnp.where(iota((2 * slots, STAT), 1) == 0, top, both)
    pay_ref[...] = full.astype(BF)


def gelu_parts(u):
    cdf = 0.5 * (1.0 + lax.erf(u * 0.7071067811865476))
    pdf = 0.3989422804014327 * jnp.exp(-0.5 * u * u)
    return u * cdf, cdf + u * pdf


def experts(own_ref, a_ref, b_ref, c_ref, win_ref, wout_ref, *out_refs):
    blocks = [r[...].astype(F32) for r in (own_ref, a_ref, b_ref, c_ref)]
    fwd = jnp.concatenate([x[:4] for x in blocks], axis=0).astype(BF)
    bwd = jnp.concatenate([x[4:] for x in blocks], axis=0).astype(BF)
    rows = fwd.shape[0]
    out, back = 0.0, 0.0
    for e in range(win_ref.shape[0]):
        mine = (iota((rows, 1), 0) % 4) // 2 == e
        w1, w2 = win_ref[e], wout_ref[e]
        gelu, slope = gelu_parts(dot(fwd, w1))
        out += dot(jnp.where(mine, gelu, 0.0).astype(BF), w2)
        dact = dot(bwd, w2, ((1,), (1,)))
        back += dot(jnp.where(mine, dact * slope, 0.0).astype(BF), w1, ((1,), (1,)))
    for v, ref in enumerate(out_refs):
        ref[...] = jnp.concatenate([out[4 * v:4 * v + 4], back[4 * v:4 * v + 4]], axis=0).astype(BF)


def finish_slots(own_ref, a_ref, b_ref, c_ref, full_ref, side_ref, out_ref):
    own, a, b, c = [r[...].astype(F32) for r in (own_ref, a_ref, b_ref, c_ref)]
    value = (own + a) + (b + c)
    width = value.shape[1]
    slots = value.shape[0] // 2
    first = iota((2 * slots, 1), 0) < slots
    side = side_ref[...]
    body = jnp.where(first, value, value / side[:, 1:2]).astype(BF)
    wide = body.astype(F32)
    shift = jnp.sum(full_ref[:slots, :] * wide[slots:, :], axis=1, keepdims=True)
    shift = jnp.concatenate([shift, shift], axis=0)
    high, low = split(shift)
    st = stats(iota((2 * slots, STAT), 1), side[:, 0:1], high, low).astype(BF)
    block = jnp.concatenate([body, st], axis=1)
    out_ref[...] = jnp.broadcast_to(block[None], out_ref.shape)


def token_grads(logit_ref, tok_ref, cot_ref, own_ref, oth_ref,
                keep_ref, send_ref, dlog_ref, dexp_ref, comb_ref, so_ref, sc_ref):
    core = lax.axis_index("c")
    logits, tok = logit_ref[...], tok_ref[...]
    n = logits.shape[1]
    width = tok.shape[1]
    zero = core == 0
    upper = iota((1, 8, 1), 1) < 4
    own, oth = own_ref[...].astype(F32), oth_ref[...].astype(F32)
    even, odd = jnp.where(zero, own, oth), jnp.where(zero, oth, own)
    first = jnp.where(upper, even, swap_halves(odd)).reshape(n, width + STAT)
    second = jnp.where(upper, swap_halves(even), odd).reshape(n, width + STAT)
    slot_out, scaled = first[:, :width].astype(BF), second[:, :width].astype(BF)
    so_ref[...] = slot_out
    sc_ref[...] = scaled
    side = first[:, width:].T
    point, shift = side[0:1, :], side[1:2, :] + side[2:3, :]
    comb = softmax_rows(logits)
    comb_ref[...] = comb.astype(BF)
    dexp = jnp.exp(logits - point).astype(BF)
    dexp_ref[...] = dexp
    dcomb = dot(cot_ref[...], slot_out, ((1,), (1,)))
    inner = dot(tok, scaled, ((1,), (1,)))
    dlog = comb * (dcomb - jnp.sum(comb * dcomb, axis=1, keepdims=True))
    dlog = (dlog + dexp.astype(F32) * (inner - shift)).astype(BF)
    dlog_ref[...] = dlog
    gp = dot(tok, dlog, ((0,), (0,))).reshape(width // 8, 8, n)
    left, right = gp[:, :, :n // 2], gp[:, :, n // 2:]
    even = jnp.where(upper, left, swap_halves(right)).astype(BF)
    odd = jnp.where(upper, swap_halves(left), right).astype(BF)
    keep_ref[...] = jnp.where(zero, even, odd).reshape(keep_ref.shape)
    send_ref[...] = jnp.where(zero, odd, even).reshape(send_ref.shape)


def token_outputs(comb_ref, so_ref, dlog_ref, par_ref, dexp_ref, sc_ref, mixed_ref, grad_ref):
    mixed_ref[...] = dot(comb_ref[...], so_ref[...]).astype(BF)
    grad = dot(dlog_ref[...], par_ref[...], ((1,), (1,)))
    grad_ref[...] = (grad + dot(dexp_ref[...], sc_ref[...])).astype(BF)


def add_halves(a_ref, b_ref, *out_refs):
    here = lax.axis_index("x")
    for k, ref in enumerate(out_refs):
        to = lax.rem(here + k, len(out_refs))
        ref[...] = (a_ref[to].astype(F32) + b_ref[to].astype(F32)).astype(BF)


def add_rows(own_ref, a_ref, b_ref, c_ref, after_ref, out_ref):
    del after_ref
    pairs = [r[...].astype(F32) for r in (own_ref, a_ref, b_ref, c_ref)]
    out_ref[...] = ((pairs[0] + pairs[1]) + (pairs[2] + pairs[3])).astype(BF)


def sum_pieces(in_ref, out_ref):
    value = in_ref[...].astype(F32)
    count, rows, half = value.shape
    total = jnp.sum(jnp.sum(value.reshape(count // 8, 8, rows, half), axis=0), axis=0)
    out_ref[:, :half] = total[:4]
    out_ref[:, half:] = total[4:]


def shifted(value, step, size):
    return lax.ppermute(value, "x", [(i, (i + step) % size) for i in range(size)])


def on_device(tokens, slot_parameters, w_in, w_out, grad_out):
    shape = jax.ShapeDtypeStruct
    tok, cot = tokens[0], grad_out[0]
    count, width = tok.shape
    n = slot_parameters.shape[1]
    videos = lax.axis_size("x")
    depth, rows_y = lax.axis_size("z"), lax.axis_size("y")
    owners = depth * rows_y
    wide = width + STAT
    unit = 2 * count * width * n
    swap = [(0, 1), (1, 0)]

    vmem = pl.BlockSpec(memory_space=pltpu.VMEM)
    keep, send, logits = pl.pallas_call(
        reduce_tokens,
        out_shape=[shape((rows_y, depth, 8, wide), BF), shape((rows_y, depth, 8, wide), BF), shape((count, n), F32)],
        in_specs=[pl.BlockSpec(memory_space=pltpu.HBM)] * 3,
        out_specs=[vmem] * 3,
        scratch_shapes=[
            pltpu.VMEM((count, width), BF), pltpu.VMEM((count, width), BF),
            pltpu.VMEM((width, n), BF), pltpu.VMEM((count, n), BF),
            pltpu.SemaphoreType.DMA((PARTS + 2,)),
        ],
        compiler_params=PARAMS,
        cost_estimate=pl.CostEstimate(flops=4 * unit, bytes_accessed=4 << 20, transcendentals=0),
    )(*[pltpu.with_memory_space_constraint(a, pltpu.HBM) for a in (tok, cot, slot_parameters)])
    other = lax.ppermute(send, "c", swap)
    (merged,) = call(merge_cores, [shape(keep.shape, BF)], keep, other, flops=40 * unit)
    columns = lax.all_to_all(merged, "y", 0, 0, tiled=True)
    (merged,) = call(merge_columns, [shape((depth, 8, wide), BF)], columns)
    shards = lax.all_to_all(merged, "z", 0, 0, tiled=True)
    pay, full, side = call(
        merge_shards,
        [shape((8, width), BF), shape((8, width), F32), shape((8, STAT), F32)],
        shards,
    )
    behind = [shifted(pay, k, videos) for k in range(1, videos)]
    partial = call(
        experts, [shape((8, width), BF)] * videos, pay, *behind, w_in, w_out,
        flops=32 * videos * w_in.size,
    )
    parts = [shifted(partial[k], -k, videos) for k in range(1, videos)]
    (block,) = call(finish_slots, [shape((owners, 8, wide), BF)], partial[0], *parts, full, side)
    mine = lax.all_to_all(block, ZY, 0, 0, tiled=True)
    theirs = lax.ppermute(mine, "c", swap)

    gp_keep, gp_send, dlog, dexp, comb, slot_out, scaled = call(
        token_grads,
        [shape((videos, owners, 8, n // 2), BF), shape((videos, owners, 8, n // 2), BF),
         shape((count, n), BF), shape((count, n), BF), shape((count, n), BF),
         shape((n, width), BF), shape((n, width), BF)],
        logits, tok, cot, mine, theirs, flops=5 * unit,
    )
    gp_other = lax.ppermute(gp_send, "c", swap)
    mixed, grad_tokens = call(
        token_outputs,
        [shape((count, width), BF), shape((count, width), BF)],
        comb, slot_out, dlog, slot_parameters, dexp, scaled, flops=3 * unit,
    )
    quarters = call(add_halves, [shape(gp_keep.shape[1:], BF)] * videos, gp_keep, gp_other)
    arrived = [shifted(quarters[k], k, videos) for k in range(1, videos)]
    half = pl.pallas_call(
        add_rows,
        out_shape=shape(gp_keep.shape[1:], BF),
        in_specs=[vmem] * videos + [pl.BlockSpec(memory_space=pltpu.HBM)],
        out_specs=vmem,
        compiler_params=PARAMS,
    )(quarters[0], *arrived, pltpu.with_memory_space_constraint(mixed, pltpu.HBM))
    pieces = lax.all_to_all(half, ZY, 0, 0, tiled=True)
    (grad_params,) = call(sum_pieces, [shape((4, n), F32)], pieces)
    return mixed[None], grad_tokens[None], grad_params


def solution(mesh):
    sizes = dict(mesh.shape)
    grid = Mesh(mesh.devices.reshape(sizes["batch"], sizes["seq"] // 8, 4, 2), AXES)
    seq = ("z", "y", "c")
    placed = (
        P("x", seq, None),
        P(),
        P(seq, None, "x"),
        P(seq, "x", None),
        P("x", seq, None),
    )
    return jax.shard_map(
        on_device,
        mesh=grid,
        in_specs=placed,
        out_specs=(P("x", seq, None), P("x", seq, None), P(AXES, None)),
        check_vma=False,
    )
```

```python
import math

import jax
import jax.numpy as jnp
from jax import lax
from jax.experimental import pallas as pl
from jax.experimental.pallas import tpu as pltpu
from jax.sharding import Mesh, PartitionSpec as P

BF = jnp.bfloat16
F32 = jnp.float32
AXES = ("x", "z", "y", "c")
ZY = ("z", "y")
PARTS = 2
STAT = 128
PARAMS = pltpu.CompilerParams(vmem_limit_bytes=24 * 1024 * 1024)


def dot(a, b, contract=((1,), (0,))):
    return lax.dot_general(a, b, (contract, ((), ())), preferred_element_type=F32)


def iota(shape, dim):
    return lax.broadcasted_iota(jnp.int32, shape, dim)


def call(body, outs, *args, flops=0, scratch=(), params=PARAMS):
    nbytes = sum(a.size * a.dtype.itemsize for a in args)
    nbytes += sum(math.prod(o.shape) * 4 for o in outs)
    return pl.pallas_call(
        body,
        out_shape=outs,
        in_specs=[pl.BlockSpec(memory_space=pltpu.VMEM)] * len(args),
        out_specs=[pl.BlockSpec(memory_space=pltpu.VMEM)] * len(outs),
        scratch_shapes=list(scratch),
        compiler_params=params,
        cost_estimate=pl.CostEstimate(flops=flops, bytes_accessed=nbytes, transcendentals=0),
    )(*args)


def split(value):
    high = value.astype(BF).astype(F32)
    return high, (value - high).astype(BF).astype(F32)


def stats(lane, first, second, third):
    return jnp.where(lane == 0, first, jnp.where(lane == 1, second, jnp.where(lane == 2, third, 0.0)))


def softmax_rows(logits):
    e = jnp.exp(logits - jnp.max(logits, axis=1, keepdims=True))
    return e / jnp.sum(e, axis=1, keepdims=True)


def swap_halves(value):
    return pltpu.roll(value, 4, 1)


def reduce_tokens(tok_hbm, cot_hbm, par_hbm, keep_ref, send_ref, logit_ref,
                  tok_ref, cot_ref, par_ref, comb_ref, sems):
    core = lax.axis_index("c")
    count, width = tok_ref.shape
    n = par_ref.shape[1]
    part = count // PARTS
    copies = [pltpu.make_async_copy(par_hbm, par_ref, sems.at[0])]
    for i in range(PARTS):
        rows = pl.ds(i * part, part)
        copies.append(pltpu.make_async_copy(tok_hbm.at[rows], tok_ref.at[rows], sems.at[1 + i]))
    copies.append(pltpu.make_async_copy(cot_hbm, cot_ref, sems.at[1 + PARTS]))
    for copy in copies:
        copy.start()
    copies[0].wait()
    par = par_ref[...]
    peak = None
    for i in range(PARTS):
        rows = pl.ds(i * part, part)
        copies[1 + i].wait()
        piece = dot(tok_ref[rows, :], par)
        logit_ref[rows, :] = piece
        comb_ref[rows, :] = softmax_rows(piece).astype(BF)
        high = jnp.max(piece, axis=0, keepdims=True)
        peak = high if peak is None else jnp.maximum(peak, high)
    refpoint = peak.astype(BF).astype(F32)
    dexp = jnp.exp(logit_ref[...] - refpoint).astype(BF)
    numer = dot(dexp, tok_ref[...], ((0,), (0,))).reshape(n // 8, 8, width)
    total = dot(dexp, jnp.ones((count, STAT), BF), ((0,), (0,)))
    diag = jnp.where(iota((n, n), 0) == iota((n, n), 1), refpoint, 0.0).astype(BF)
    point = dot(diag, jnp.ones((n, STAT), BF))
    high, low = split(total)
    side = stats(iota((n, STAT), 1), point, high, low).reshape(n // 8, 8, STAT)
    copies[1 + PARTS].wait()
    dslot = dot(comb_ref[...], cot_ref[...], ((0,), (0,))).reshape(n // 8, 8, width)
    upper = iota((1, 8, 1), 1) < 4
    zero = core == 0
    even = jnp.where(upper, numer, swap_halves(dslot)).astype(BF)
    odd = jnp.where(upper, swap_halves(numer), dslot).astype(BF)
    even_side = jnp.where(upper, side, 0.0).astype(BF)
    odd_side = jnp.where(upper, swap_halves(side), 0.0).astype(BF)
    even = jnp.concatenate([even, even_side], axis=2)
    odd = jnp.concatenate([odd, odd_side], axis=2)
    for ref, value in ((keep_ref, jnp.where(zero, even, odd)), (send_ref, jnp.where(zero, odd, even))):
        value = value.reshape(n // 8 // ref.shape[0], *ref.shape[:1], 8, width + STAT)
        for y in range(ref.shape[0]):
            ref[y] = value[:, y]


def merge(parts):
    width = parts[0].shape[-1] - STAT
    points = [p[..., width:width + 1] for p in parts]
    top = points[0]
    for point in points[1:]:
        top = jnp.maximum(top, point)
    body, total = 0.0, 0.0
    for part, point in zip(parts, points):
        scale = jnp.exp(point - top)
        body += scale * part[..., :width]
        total += scale * (part[..., width + 1:width + 2] + part[..., width + 2:width + 3])
    return body, top, total


def store_merged(parts, out_ref):
    body, top, total = merge(parts)
    width = body.shape[-1]
    high, low = split(total)
    out_ref[..., :width] = body.astype(BF)
    lane = iota(body.shape[:-1] + (STAT,), body.ndim - 1)
    out_ref[..., width:] = stats(lane, top, high, low).astype(BF)


def merge_cores(a_ref, b_ref, *out_refs):
    here = lax.axis_index("y")
    for k, ref in enumerate(out_refs):
        to = lax.rem(here + k, len(out_refs))
        store_merged([a_ref[to].astype(F32), b_ref[to].astype(F32)], ref)


def merge_columns(a_ref, b_ref, c_ref, d_ref, out_ref):
    store_merged([r[...].astype(F32) for r in (a_ref, b_ref, c_ref, d_ref)], out_ref)


def merge_shards(in_ref, pay_ref, full_ref, side_ref):
    acc, top, total = merge([in_ref[i].astype(F32) for i in range(in_ref.shape[0])])
    slots = acc.shape[0] // 2
    first = iota((2 * slots, 1), 0) < slots
    full = acc / jnp.where(first, total, 1.0)
    full_ref[...] = full
    both = jnp.concatenate([total[:slots], total[:slots]], axis=0)
    side_ref[...] = jnp.where(iota((2 * slots, STAT), 1) == 0, top, both)
    pay_ref[...] = full.astype(BF)


def gelu_parts(u):
    cdf = 0.5 * (1.0 + lax.erf(u * 0.7071067811865476))
    pdf = 0.3989422804014327 * jnp.exp(-0.5 * u * u)
    return u * cdf, cdf + u * pdf


def experts(own_ref, a_ref, b_ref, c_ref, win_ref, wout_ref, *out_refs):
    blocks = [r[...].astype(F32) for r in (own_ref, a_ref, b_ref, c_ref)]
    fwd = jnp.concatenate([x[:4] for x in blocks], axis=0).astype(BF)
    bwd = jnp.concatenate([x[4:] for x in blocks], axis=0).astype(BF)
    rows = fwd.shape[0]
    out, back = 0.0, 0.0
    for e in range(win_ref.shape[0]):
        mine = (iota((rows, 1), 0) % 4) // 2 == e
        w1, w2 = win_ref[e], wout_ref[e]
        gelu, slope = gelu_parts(dot(fwd, w1))
        out += dot(jnp.where(mine, gelu, 0.0).astype(BF), w2)
        dact = dot(bwd, w2, ((1,), (1,)))
        back += dot(jnp.where(mine, dact * slope, 0.0).astype(BF), w1, ((1,), (1,)))
    for v, ref in enumerate(out_refs):
        ref[...] = jnp.concatenate([out[4 * v:4 * v + 4], back[4 * v:4 * v + 4]], axis=0).astype(BF)


def finish_slots(own_ref, a_ref, b_ref, c_ref, full_ref, side_ref, out_ref):
    own, a, b, c = [r[...].astype(F32) for r in (own_ref, a_ref, b_ref, c_ref)]
    value = (own + a) + (b + c)
    width = value.shape[1]
    slots = value.shape[0] // 2
    first = iota((2 * slots, 1), 0) < slots
    side = side_ref[...]
    body = jnp.where(first, value, value / side[:, 1:2]).astype(BF)
    wide = body.astype(F32)
    shift = jnp.sum(full_ref[:slots, :] * wide[slots:, :], axis=1, keepdims=True)
    shift = jnp.concatenate([shift, shift], axis=0)
    high, low = split(shift)
    st = stats(iota((2 * slots, STAT), 1), side[:, 0:1], high, low).astype(BF)
    block = jnp.concatenate([body, st], axis=1)
    out_ref[...] = jnp.broadcast_to(block[None], out_ref.shape)


def token_grads(logit_ref, tok_ref, cot_ref, own_ref, oth_ref,
                keep_ref, send_ref, dlog_ref, dexp_ref, comb_ref, so_ref, sc_ref):
    core = lax.axis_index("c")
    logits, tok = logit_ref[...], tok_ref[...]
    n = logits.shape[1]
    width = tok.shape[1]
    zero = core == 0
    upper = iota((1, 8, 1), 1) < 4
    own, oth = own_ref[...].astype(F32), oth_ref[...].astype(F32)
    even, odd = jnp.where(zero, own, oth), jnp.where(zero, oth, own)
    first = jnp.where(upper, even, swap_halves(odd)).reshape(n, width + STAT)
    second = jnp.where(upper, swap_halves(even), odd).reshape(n, width + STAT)
    slot_out, scaled = first[:, :width].astype(BF), second[:, :width].astype(BF)
    so_ref[...] = slot_out
    sc_ref[...] = scaled
    side = first[:, width:].T
    point, shift = side[0:1, :], side[1:2, :] + side[2:3, :]
    comb = softmax_rows(logits)
    comb_ref[...] = comb.astype(BF)
    dexp = jnp.exp(logits - point).astype(BF)
    dexp_ref[...] = dexp
    dcomb = dot(cot_ref[...], slot_out, ((1,), (1,)))
    inner = dot(tok, scaled, ((1,), (1,)))
    dlog = comb * (dcomb - jnp.sum(comb * dcomb, axis=1, keepdims=True))
    dlog = (dlog + dexp.astype(F32) * (inner - shift)).astype(BF)
    dlog_ref[...] = dlog
    gp = dot(tok, dlog, ((0,), (0,))).reshape(width // 8, 8, n)
    left, right = gp[:, :, :n // 2], gp[:, :, n // 2:]
    even = jnp.where(upper, left, swap_halves(right)).astype(BF)
    odd = jnp.where(upper, swap_halves(left), right).astype(BF)
    keep_ref[...] = jnp.where(zero, even, odd).reshape(keep_ref.shape)
    send_ref[...] = jnp.where(zero, odd, even).reshape(send_ref.shape)


def token_outputs(comb_ref, so_ref, dlog_ref, par_ref, dexp_ref, sc_ref, mixed_ref, grad_ref):
    mixed_ref[...] = dot(comb_ref[...], so_ref[...]).astype(BF)
    grad = dot(dlog_ref[...], par_ref[...], ((1,), (1,)))
    grad_ref[...] = (grad + dot(dexp_ref[...], sc_ref[...])).astype(BF)


def add_halves(a_ref, b_ref, *out_refs):
    here = lax.axis_index("x")
    for k, ref in enumerate(out_refs):
        to = lax.rem(here + k, len(out_refs))
        ref[...] = (a_ref[to].astype(F32) + b_ref[to].astype(F32)).astype(BF)


def add_rows(own_ref, a_ref, b_ref, c_ref, after_ref, out_ref):
    del after_ref
    pairs = [r[...].astype(F32) for r in (own_ref, a_ref, b_ref, c_ref)]
    out_ref[...] = ((pairs[0] + pairs[1]) + (pairs[2] + pairs[3])).astype(BF)


def sum_pieces(in_ref, out_ref):
    value = in_ref[...].astype(F32)
    count, rows, half = value.shape
    total = jnp.sum(jnp.sum(value.reshape(count // 8, 8, rows, half), axis=0), axis=0)
    out_ref[:, :half] = total[:4]
    out_ref[:, half:] = total[4:]


def shifted(value, step, size, axis="x"):
    return lax.ppermute(value, axis, [(i, (i + step) % size) for i in range(size)])


def on_device(tokens, slot_parameters, w_in, w_out, grad_out):
    shape = jax.ShapeDtypeStruct
    tok, cot = tokens[0], grad_out[0]
    count, width = tok.shape
    n = slot_parameters.shape[1]
    videos = lax.axis_size("x")
    depth, rows_y = lax.axis_size("z"), lax.axis_size("y")
    owners = depth * rows_y
    wide = width + STAT
    unit = 2 * count * width * n
    swap = [(0, 1), (1, 0)]

    vmem = pl.BlockSpec(memory_space=pltpu.VMEM)
    keep, send, logits = pl.pallas_call(
        reduce_tokens,
        out_shape=[shape((rows_y, depth, 8, wide), BF), shape((rows_y, depth, 8, wide), BF), shape((count, n), F32)],
        in_specs=[pl.BlockSpec(memory_space=pltpu.HBM)] * 3,
        out_specs=[vmem] * 3,
        scratch_shapes=[
            pltpu.VMEM((count, width), BF), pltpu.VMEM((count, width), BF),
            pltpu.VMEM((width, n), BF), pltpu.VMEM((count, n), BF),
            pltpu.SemaphoreType.DMA((PARTS + 2,)),
        ],
        compiler_params=PARAMS,
        cost_estimate=pl.CostEstimate(flops=4 * unit, bytes_accessed=4 << 20, transcendentals=0),
    )(*[pltpu.with_memory_space_constraint(a, pltpu.HBM) for a in (tok, cot, slot_parameters)])
    other = lax.ppermute(send, "c", swap)
    blocks = call(merge_cores, [shape((depth, 8, wide), BF)] * rows_y, keep, other, flops=40 * unit)
    columns = [shifted(blocks[k], k, rows_y, "y") for k in range(1, rows_y)]
    (merged,) = call(merge_columns, [shape((depth, 8, wide), BF)], blocks[0], *columns)
    shards = lax.all_to_all(merged, "z", 0, 0, tiled=True)
    pay, full, side = call(
        merge_shards,
        [shape((8, width), BF), shape((8, width), F32), shape((8, STAT), F32)],
        shards,
    )
    behind = [shifted(pay, k, videos) for k in range(1, videos)]
    partial = call(
        experts, [shape((8, width), BF)] * videos, pay, *behind, w_in, w_out,
        flops=32 * videos * w_in.size,
    )
    parts = [shifted(partial[k], -k, videos) for k in range(1, videos)]
    (block,) = call(finish_slots, [shape((owners, 8, wide), BF)], partial[0], *parts, full, side)
    mine = lax.all_to_all(block, ZY, 0, 0, tiled=True)
    theirs = lax.ppermute(mine, "c", swap)

    gp_keep, gp_send, dlog, dexp, comb, slot_out, scaled = call(
        token_grads,
        [shape((videos, owners, 8, n // 2), BF), shape((videos, owners, 8, n // 2), BF),
         shape((count, n), BF), shape((count, n), BF), shape((count, n), BF),
         shape((n, width), BF), shape((n, width), BF)],
        logits, tok, cot, mine, theirs, flops=5 * unit,
    )
    gp_other = lax.ppermute(gp_send, "c", swap)
    mixed, grad_tokens = call(
        token_outputs,
        [shape((count, width), BF), shape((count, width), BF)],
        comb, slot_out, dlog, slot_parameters, dexp, scaled, flops=3 * unit,
    )
    quarters = call(add_halves, [shape(gp_keep.shape[1:], BF)] * videos, gp_keep, gp_other)
    arrived = [shifted(quarters[k], k, videos) for k in range(1, videos)]
    half = pl.pallas_call(
        add_rows,
        out_shape=shape(gp_keep.shape[1:], BF),
        in_specs=[vmem] * videos + [pl.BlockSpec(memory_space=pltpu.HBM)],
        out_specs=vmem,
        compiler_params=PARAMS,
    )(quarters[0], *arrived, pltpu.with_memory_space_constraint(mixed, pltpu.HBM))
    pieces = lax.all_to_all(half, ZY, 0, 0, tiled=True)
    (grad_params,) = call(sum_pieces, [shape((4, n), F32)], pieces)
    return mixed[None], grad_tokens[None], grad_params


def solution(mesh):
    sizes = dict(mesh.shape)
    grid = Mesh(mesh.devices.reshape(sizes["batch"], sizes["seq"] // 8, 4, 2), AXES)
    seq = ("z", "y", "c")
    placed = (
        P("x", seq, None),
        P(),
        P(seq, None, "x"),
        P(seq, "x", None),
        P("x", seq, None),
    )
    return jax.shard_map(
        on_device,
        mesh=grid,
        in_specs=placed,
        out_specs=(P("x", seq, None), P("x", seq, None), P(AXES, None)),
        check_vma=False,
    )
```

```python
import math

import jax
import jax.numpy as jnp
from jax import lax
from jax.experimental import pallas as pl
from jax.experimental.pallas import tpu as pltpu
from jax.sharding import Mesh, PartitionSpec as P

BF = jnp.bfloat16
F32 = jnp.float32
AXES = ("x", "z", "y", "c")
ZY = ("z", "y")
PARTS = 2
STAT = 128
PARAMS = pltpu.CompilerParams(vmem_limit_bytes=24 * 1024 * 1024)


def dot(a, b, contract=((1,), (0,))):
    return lax.dot_general(a, b, (contract, ((), ())), preferred_element_type=F32)


def iota(shape, dim):
    return lax.broadcasted_iota(jnp.int32, shape, dim)


def call(body, outs, *args, flops=0, scratch=(), params=PARAMS):
    nbytes = sum(a.size * a.dtype.itemsize for a in args)
    nbytes += sum(math.prod(o.shape) * 4 for o in outs)
    return pl.pallas_call(
        body,
        out_shape=outs,
        in_specs=[pl.BlockSpec(memory_space=pltpu.VMEM)] * len(args),
        out_specs=[pl.BlockSpec(memory_space=pltpu.VMEM)] * len(outs),
        scratch_shapes=list(scratch),
        compiler_params=params,
        cost_estimate=pl.CostEstimate(flops=flops, bytes_accessed=nbytes, transcendentals=0),
    )(*args)


def split(value):
    high = value.astype(BF).astype(F32)
    return high, (value - high).astype(BF).astype(F32)


def stats(lane, first, second, third):
    return jnp.where(lane == 0, first, jnp.where(lane == 1, second, jnp.where(lane == 2, third, 0.0)))


def softmax_rows(logits):
    e = jnp.exp(logits - jnp.max(logits, axis=1, keepdims=True))
    return e / jnp.sum(e, axis=1, keepdims=True)


def swap_halves(value):
    return pltpu.roll(value, 4, 1)


def reduce_tokens(tok_hbm, cot_hbm, par_hbm, *refs):
    *refs, logit_ref, tok_ref, cot_ref, par_ref, comb_ref, all_ref, sems = refs
    core = lax.axis_index("c")
    count, width = tok_ref.shape
    n = par_ref.shape[1]
    part = count // PARTS
    copies = [pltpu.make_async_copy(par_hbm, par_ref, sems.at[0])]
    for i in range(PARTS):
        rows = pl.ds(i * part, part)
        copies.append(pltpu.make_async_copy(tok_hbm.at[rows], tok_ref.at[rows], sems.at[1 + i]))
    copies.append(pltpu.make_async_copy(cot_hbm, cot_ref, sems.at[1 + PARTS]))
    for copy in copies:
        copy.start()
    copies[0].wait()
    par = par_ref[...]
    peak = None
    for i in range(PARTS):
        rows = pl.ds(i * part, part)
        copies[1 + i].wait()
        piece = dot(tok_ref[rows, :], par)
        logit_ref[rows, :] = piece
        comb_ref[rows, :] = softmax_rows(piece).astype(BF)
        high = jnp.max(piece, axis=0, keepdims=True)
        peak = high if peak is None else jnp.maximum(peak, high)
    refpoint = peak.astype(BF).astype(F32)
    dexp = jnp.exp(logit_ref[...] - refpoint).astype(BF)
    numer = dot(dexp, tok_ref[...], ((0,), (0,))).reshape(n // 8, 8, width)
    total = dot(dexp, jnp.ones((count, STAT), BF), ((0,), (0,)))
    diag = jnp.where(iota((n, n), 0) == iota((n, n), 1), refpoint, 0.0).astype(BF)
    point = dot(diag, jnp.ones((n, STAT), BF))
    high, low = split(total)
    copies[1 + PARTS].wait()
    dslot = dot(comb_ref[...], cot_ref[...], ((0,), (0,))).reshape(n // 8, 8, width)
    upper = iota((1, 8, 1), 1) < 4
    zero = core == 0
    even = jnp.where(upper, numer, swap_halves(dslot)).astype(BF)
    odd = jnp.where(upper, swap_halves(numer), dslot).astype(BF)
    sides = [value.reshape(n // 8, 8, STAT) for value in (point, high, low)]
    even_sides = [jnp.where(upper, value, 0.0) for value in sides]
    odd_sides = [jnp.where(upper, swap_halves(value), 0.0) for value in sides]
    columns = all_ref.shape[1]
    depth = n // 8 // columns
    keep = jnp.where(zero, even, odd)
    send = jnp.where(zero, odd, even)
    keep_sides = [jnp.where(zero, e, o) for e, o in zip(even_sides, odd_sides)]
    send_sides = [jnp.where(zero, o, e) for e, o in zip(even_sides, odd_sides)]
    lane = iota((8, STAT), 1)
    for which, (value, marks) in enumerate(((keep, keep_sides), (send, send_sides))):
        for y in range(columns):
            for z in range(depth):
                for j in range(width // STAT):
                    all_ref[which, y, z * (width // STAT) + j] = value[z * columns + y, :, j * STAT:(j + 1) * STAT]
            tile = jnp.zeros((8, STAT), F32)
            for i, mark in enumerate(marks):
                for z in range(depth):
                    tile = jnp.where(lane == i * depth + z, mark[z * columns + y], tile)
            all_ref[which, y, depth * (width // STAT)] = tile.astype(BF)
    here = lax.axis_index("y")
    for k in range(columns):
        to = lax.rem(here + k, columns)
        refs[k][...] = all_ref[0, to]
        refs[columns + k][...] = all_ref[1, to]


def merge_tiles(parts):
    count = parts[0].shape[0] - 1
    groups = 8
    marks = [p[count].astype(F32) for p in parts]
    top = marks[0]
    for mark in marks[1:]:
        top = jnp.maximum(top, mark)
    scales = [jnp.exp(mark - top) for mark in marks]
    total = 0.0
    for scale, mark in zip(scales, marks):
        total += scale * (pltpu.roll(mark, STAT - groups, 1) + pltpu.roll(mark, STAT - 2 * groups, 1))
    size = count // groups
    bodies = []
    for z in range(groups):
        body = 0.0
        for scale, part in zip(scales, parts):
            body += scale[:, z:z + 1][None] * part[z * size:(z + 1) * size].astype(F32)
        bodies.append(body.astype(BF))
    high, low = split(total)
    return bodies, top, high, low


def merge_cores(a_ref, b_ref, out_ref):
    bodies, top, high, low = merge_tiles([a_ref, b_ref])
    size = bodies[0].shape[0]
    for z, body in enumerate(bodies):
        out_ref[z * size:(z + 1) * size] = body
    lane = iota(top.shape, 1)
    mark = jnp.where(lane < 16, pltpu.roll(high, 8, 1), jnp.where(lane < 24, pltpu.roll(low, 16, 1), 0.0))
    out_ref[len(bodies) * size] = jnp.where(lane < 8, top, mark).astype(BF)


def merge_columns(a_ref, b_ref, c_ref, d_ref, out_ref):
    bodies, top, high, low = merge_tiles([a_ref, b_ref, c_ref, d_ref])
    size = bodies[0].shape[0]
    lane = iota(top.shape, 1)
    for z, body in enumerate(bodies):
        out_ref[z, :size] = body
        out_ref[z, size] = stats(lane, top[:, z:z + 1], high[:, z:z + 1], low[:, z:z + 1]).astype(BF)


def merge_shards(in_ref, pay_ref, full_ref, side_ref):
    size = in_ref.shape[1] - 1
    marks = [in_ref[i, size].astype(F32) for i in range(in_ref.shape[0])]
    top = marks[0][:, 0:1]
    for mark in marks[1:]:
        top = jnp.maximum(top, mark[:, 0:1])
    acc, total = 0.0, 0.0
    for i, mark in enumerate(marks):
        scale = jnp.exp(mark[:, 0:1] - top)
        acc += scale[None] * in_ref[i, :size].astype(F32)
        total += scale * (mark[:, 1:2] + mark[:, 2:3])
    slots = total.shape[0] // 2
    first = iota((2 * slots, 1), 0) < slots
    full = acc / jnp.where(first, total, 1.0)[None]
    for j in range(size):
        full_ref[:, j * STAT:(j + 1) * STAT] = full[j]
        pay_ref[:, j * STAT:(j + 1) * STAT] = full[j].astype(BF)
    both = jnp.concatenate([total[:slots], total[:slots]], axis=0)
    side_ref[...] = jnp.where(iota((2 * slots, STAT), 1) == 0, top, both)


def gelu_parts(u):
    cdf = 0.5 * (1.0 + lax.erf(u * 0.7071067811865476))
    pdf = 0.3989422804014327 * jnp.exp(-0.5 * u * u)
    return u * cdf, cdf + u * pdf


def experts(own_ref, a_ref, b_ref, c_ref, win_ref, wout_ref, *out_refs):
    blocks = [r[...].astype(F32) for r in (own_ref, a_ref, b_ref, c_ref)]
    fwd = jnp.concatenate([x[:4] for x in blocks], axis=0).astype(BF)
    bwd = jnp.concatenate([x[4:] for x in blocks], axis=0).astype(BF)
    rows = fwd.shape[0]
    out, back = 0.0, 0.0
    for e in range(win_ref.shape[0]):
        mine = (iota((rows, 1), 0) % 4) // 2 == e
        w1, w2 = win_ref[e], wout_ref[e]
        gelu, slope = gelu_parts(dot(fwd, w1))
        out += dot(jnp.where(mine, gelu, 0.0).astype(BF), w2)
        dact = dot(bwd, w2, ((1,), (1,)))
        back += dot(jnp.where(mine, dact * slope, 0.0).astype(BF), w1, ((1,), (1,)))
    for v, ref in enumerate(out_refs):
        ref[...] = jnp.concatenate([out[4 * v:4 * v + 4], back[4 * v:4 * v + 4]], axis=0).astype(BF)


def finish_slots(own_ref, a_ref, b_ref, c_ref, full_ref, side_ref, out_ref):
    own, a, b, c = [r[...].astype(F32) for r in (own_ref, a_ref, b_ref, c_ref)]
    value = (own + a) + (b + c)
    width = value.shape[1]
    slots = value.shape[0] // 2
    first = iota((2 * slots, 1), 0) < slots
    side = side_ref[...]
    body = jnp.where(first, value, value / side[:, 1:2]).astype(BF)
    wide = body.astype(F32)
    shift = jnp.sum(full_ref[:slots, :] * wide[slots:, :], axis=1, keepdims=True)
    shift = jnp.concatenate([shift, shift], axis=0)
    high, low = split(shift)
    st = stats(iota((2 * slots, STAT), 1), side[:, 0:1], high, low).astype(BF)
    block = jnp.concatenate([body, st], axis=1)
    out_ref[...] = jnp.broadcast_to(block[None], out_ref.shape)


def token_grads(logit_ref, tok_ref, cot_ref, own_ref, oth_ref, *refs):
    *out_refs, dlog_ref, dexp_ref, comb_ref, so_ref, sc_ref, all_ref = refs
    core = lax.axis_index("c")
    logits, tok = logit_ref[...], tok_ref[...]
    n = logits.shape[1]
    width = tok.shape[1]
    zero = core == 0
    upper = iota((1, 8, 1), 1) < 4
    own, oth = own_ref[...].astype(F32), oth_ref[...].astype(F32)
    even, odd = jnp.where(zero, own, oth), jnp.where(zero, oth, own)
    first = jnp.where(upper, even, swap_halves(odd)).reshape(n, width + STAT)
    second = jnp.where(upper, swap_halves(even), odd).reshape(n, width + STAT)
    slot_out, scaled = first[:, :width].astype(BF), second[:, :width].astype(BF)
    so_ref[...] = slot_out
    sc_ref[...] = scaled
    side = first[:, width:].T
    point, shift = side[0:1, :], side[1:2, :] + side[2:3, :]
    comb = softmax_rows(logits)
    comb_ref[...] = comb.astype(BF)
    dexp = jnp.exp(logits - point).astype(BF)
    dexp_ref[...] = dexp
    dcomb = dot(cot_ref[...], slot_out, ((1,), (1,)))
    inner = dot(tok, scaled, ((1,), (1,)))
    dlog = comb * (dcomb - jnp.sum(comb * dcomb, axis=1, keepdims=True))
    dlog = (dlog + dexp.astype(F32) * (inner - shift)).astype(BF)
    dlog_ref[...] = dlog
    gp = dot(tok, dlog, ((0,), (0,))).reshape(width // 8, 8, n)
    left, right = gp[:, :, :n // 2], gp[:, :, n // 2:]
    even = jnp.where(upper, left, swap_halves(right)).astype(BF)
    odd = jnp.where(upper, swap_halves(left), right).astype(BF)
    all_ref[0] = jnp.where(zero, even, odd).reshape(all_ref.shape[1:])
    all_ref[1] = jnp.where(zero, odd, even).reshape(all_ref.shape[1:])
    here, steps = lax.axis_index("x"), all_ref.shape[1]
    for k in range(steps):
        to = lax.rem(here + k, steps)
        out_refs[k][...] = all_ref[0, to]
        out_refs[steps + k][...] = all_ref[1, to]


def token_outputs(comb_ref, so_ref, dlog_ref, par_ref, dexp_ref, sc_ref, mixed_ref, grad_ref):
    mixed_ref[...] = dot(comb_ref[...], so_ref[...]).astype(BF)
    grad = dot(dlog_ref[...], par_ref[...], ((1,), (1,)))
    grad_ref[...] = (grad + dot(dexp_ref[...], sc_ref[...])).astype(BF)


def add_halves(a_ref, b_ref, out_ref):
    out_ref[...] = (a_ref[...].astype(F32) + b_ref[...].astype(F32)).astype(BF)


def add_rows(own_ref, a_ref, b_ref, c_ref, after_ref, out_ref):
    del after_ref
    pairs = [r[...].astype(F32) for r in (own_ref, a_ref, b_ref, c_ref)]
    out_ref[...] = ((pairs[0] + pairs[1]) + (pairs[2] + pairs[3])).astype(BF)


def sum_pieces(in_ref, out_ref):
    value = in_ref[...].astype(F32)
    count, rows, half = value.shape
    total = jnp.sum(jnp.sum(value.reshape(count // 8, 8, rows, half), axis=0), axis=0)
    out_ref[:, :half] = total[:4]
    out_ref[:, half:] = total[4:]


def shifted(value, step, size, axis="x"):
    return lax.ppermute(value, axis, [(i, (i + step) % size) for i in range(size)])


def on_device(tokens, slot_parameters, w_in, w_out, grad_out):
    shape = jax.ShapeDtypeStruct
    tok, cot = tokens[0], grad_out[0]
    count, width = tok.shape
    n = slot_parameters.shape[1]
    videos = lax.axis_size("x")
    depth, rows_y = lax.axis_size("z"), lax.axis_size("y")
    owners = depth * rows_y
    wide = width + STAT
    unit = 2 * count * width * n
    swap = [(0, 1), (1, 0)]

    vmem = pl.BlockSpec(memory_space=pltpu.VMEM)
    tiles = (depth * (width // STAT) + 1, 8, STAT)
    *blocks, logits = pl.pallas_call(
        reduce_tokens,
        out_shape=[shape(tiles, BF)] * (2 * rows_y) + [shape((count, n), F32)],
        in_specs=[pl.BlockSpec(memory_space=pltpu.HBM)] * 3,
        out_specs=[vmem] * (2 * rows_y + 1),
        scratch_shapes=[
            pltpu.VMEM((count, width), BF), pltpu.VMEM((count, width), BF),
            pltpu.VMEM((width, n), BF), pltpu.VMEM((count, n), BF),
            pltpu.VMEM((2, rows_y) + tiles, BF),
            pltpu.SemaphoreType.DMA((PARTS + 2,)),
        ],
        compiler_params=PARAMS,
        cost_estimate=pl.CostEstimate(flops=4 * unit, bytes_accessed=4 << 20, transcendentals=0),
    )(*[pltpu.with_memory_space_constraint(a, pltpu.HBM) for a in (tok, cot, slot_parameters)])
    order = sorted(range(rows_y), key=lambda k: -min(k, rows_y - k))
    others = {k: lax.ppermute(blocks[rows_y + k], "c", swap) for k in order}
    shares = {}
    for k in order:
        (share,) = call(merge_cores, [shape(tiles, BF)], blocks[k], others[k], flops=10 * unit)
        shares[k] = shifted(share, k, rows_y, "y") if k else share
    (merged,) = call(
        merge_columns, [shape((depth, width // STAT + 1, 8, STAT), BF)],
        *[shares[k] for k in range(rows_y)],
    )
    shards = lax.all_to_all(merged, "z", 0, 0, tiled=True)
    pay, full, side = call(
        merge_shards,
        [shape((8, width), BF), shape((8, width), F32), shape((8, STAT), F32)],
        shards,
    )
    behind = [shifted(pay, k, videos) for k in range(1, videos)]
    partial = call(
        experts, [shape((8, width), BF)] * videos, pay, *behind, w_in, w_out,
        flops=32 * videos * w_in.size,
    )
    parts = [shifted(partial[k], -k, videos) for k in range(1, videos)]
    (block,) = call(finish_slots, [shape((owners, 8, wide), BF)], partial[0], *parts, full, side)
    mine = lax.all_to_all(block, ZY, 0, 0, tiled=True)
    theirs = lax.ppermute(mine, "c", swap)

    quarter = shape((owners, 8, n // 2), BF)
    *quarters, dlog, dexp, comb, slot_out, scaled = call(
        token_grads,
        [quarter] * (2 * videos)
        + [shape((count, n), BF), shape((count, n), BF), shape((count, n), BF),
           shape((n, width), BF), shape((n, width), BF)],
        logits, tok, cot, mine, theirs, flops=5 * unit,
        scratch=[pltpu.VMEM((2, videos) + quarter.shape, BF)],
    )
    order = sorted(range(videos), key=lambda k: -min(k, videos - k))
    others = {k: lax.ppermute(quarters[videos + k], "c", swap) for k in order}
    shares = {}
    for k in order:
        (share,) = call(add_halves, [quarter], quarters[k], others[k])
        shares[k] = shifted(share, k, videos) if k else share
    mixed, grad_tokens = call(
        token_outputs,
        [shape((count, width), BF), shape((count, width), BF)],
        comb, slot_out, dlog, slot_parameters, dexp, scaled, flops=3 * unit,
    )
    half = pl.pallas_call(
        add_rows,
        out_shape=quarter,
        in_specs=[vmem] * videos + [pl.BlockSpec(memory_space=pltpu.HBM)],
        out_specs=vmem,
        compiler_params=PARAMS,
    )(*[shares[k] for k in range(videos)], pltpu.with_memory_space_constraint(mixed, pltpu.HBM))
    pieces = lax.all_to_all(half, ZY, 0, 0, tiled=True)
    (grad_params,) = call(sum_pieces, [shape((4, n), F32)], pieces)
    return mixed[None], grad_tokens[None], grad_params


def solution(mesh):
    sizes = dict(mesh.shape)
    grid = Mesh(mesh.devices.reshape(sizes["batch"], sizes["seq"] // 8, 4, 2), AXES)
    seq = ("z", "y", "c")
    placed = (
        P("x", seq, None),
        P(),
        P(seq, None, "x"),
        P(seq, "x", None),
        P("x", seq, None),
    )
    return jax.shard_map(
        on_device,
        mesh=grid,
        in_specs=placed,
        out_specs=(P("x", seq, None), P("x", seq, None), P(AXES, None)),
        check_vma=False,
    )
```

```python
import math

import jax
import jax.numpy as jnp
from jax import lax
from jax.experimental import pallas as pl
from jax.experimental.pallas import tpu as pltpu
from jax.sharding import Mesh, PartitionSpec as P

BF = jnp.bfloat16
F32 = jnp.float32
AXES = ("x", "z", "y", "c")
ZY = ("z", "y")
PARTS = 2
STAT = 128
PARAMS = pltpu.CompilerParams(vmem_limit_bytes=24 * 1024 * 1024)


def dot(a, b, contract=((1,), (0,))):
    return lax.dot_general(a, b, (contract, ((), ())), preferred_element_type=F32)


def iota(shape, dim):
    return lax.broadcasted_iota(jnp.int32, shape, dim)


def call(body, outs, *args, flops=0, scratch=(), params=PARAMS):
    nbytes = sum(a.size * a.dtype.itemsize for a in args)
    nbytes += sum(math.prod(o.shape) * 4 for o in outs)
    return pl.pallas_call(
        body,
        out_shape=outs,
        in_specs=[pl.BlockSpec(memory_space=pltpu.VMEM)] * len(args),
        out_specs=[pl.BlockSpec(memory_space=pltpu.VMEM)] * len(outs),
        scratch_shapes=list(scratch),
        compiler_params=params,
        cost_estimate=pl.CostEstimate(flops=flops, bytes_accessed=nbytes, transcendentals=0),
    )(*args)


def split(value):
    high = value.astype(BF).astype(F32)
    return high, (value - high).astype(BF).astype(F32)


def stats(lane, first, second, third):
    return jnp.where(lane == 0, first, jnp.where(lane == 1, second, jnp.where(lane == 2, third, 0.0)))


def softmax_rows(logits):
    e = jnp.exp(logits - jnp.max(logits, axis=1, keepdims=True))
    return e / jnp.sum(e, axis=1, keepdims=True)


def swap_halves(value):
    return pltpu.roll(value, 4, 1)


def reduce_tokens(tok_hbm, cot_hbm, par_hbm, *refs):
    *refs, logit_ref, tok_ref, cot_ref, par_ref, comb_ref, all_ref, sems = refs
    core = lax.axis_index("c")
    count, width = tok_ref.shape
    n = par_ref.shape[1]
    part = count // PARTS
    copies = [pltpu.make_async_copy(par_hbm, par_ref, sems.at[0])]
    for i in range(PARTS):
        rows = pl.ds(i * part, part)
        copies.append(pltpu.make_async_copy(tok_hbm.at[rows], tok_ref.at[rows], sems.at[1 + i]))
    copies.append(pltpu.make_async_copy(cot_hbm, cot_ref, sems.at[1 + PARTS]))
    for copy in copies:
        copy.start()
    copies[0].wait()
    par = par_ref[...]
    peak = None
    for i in range(PARTS):
        rows = pl.ds(i * part, part)
        copies[1 + i].wait()
        piece = dot(tok_ref[rows, :], par)
        logit_ref[rows, :] = piece
        comb_ref[rows, :] = softmax_rows(piece).astype(BF)
        high = jnp.max(piece, axis=0, keepdims=True)
        peak = high if peak is None else jnp.maximum(peak, high)
    refpoint = peak.astype(BF).astype(F32)
    dexp = jnp.exp(logit_ref[...] - refpoint).astype(BF)
    numer = dot(dexp, tok_ref[...], ((0,), (0,))).reshape(n // 8, 8, width)
    total = dot(dexp, jnp.ones((count, STAT), BF), ((0,), (0,)))
    diag = jnp.where(iota((n, n), 0) == iota((n, n), 1), refpoint, 0.0).astype(BF)
    point = dot(diag, jnp.ones((n, STAT), BF))
    high, low = split(total)
    copies[1 + PARTS].wait()
    dslot = dot(comb_ref[...], cot_ref[...], ((0,), (0,))).reshape(n // 8, 8, width)
    upper = iota((1, 8, 1), 1) < 4
    zero = core == 0
    even = jnp.where(upper, numer, swap_halves(dslot)).astype(BF)
    odd = jnp.where(upper, swap_halves(numer), dslot).astype(BF)
    sides = [value.reshape(n // 8, 8, STAT) for value in (point, high, low)]
    even_sides = [jnp.where(upper, value, 0.0) for value in sides]
    odd_sides = [jnp.where(upper, swap_halves(value), 0.0) for value in sides]
    columns = all_ref.shape[1]
    depth = n // 8 // columns
    keep = jnp.where(zero, even, odd)
    send = jnp.where(zero, odd, even)
    keep_sides = [jnp.where(zero, e, o) for e, o in zip(even_sides, odd_sides)]
    send_sides = [jnp.where(zero, o, e) for e, o in zip(even_sides, odd_sides)]
    lane = iota((8, STAT), 1)
    for which, (value, marks) in enumerate(((keep, keep_sides), (send, send_sides))):
        for y in range(columns):
            for z in range(depth):
                for j in range(width // STAT):
                    all_ref[which, y, z * (width // STAT) + j] = value[z * columns + y, :, j * STAT:(j + 1) * STAT]
            tile = jnp.zeros((8, STAT), F32)
            for i, mark in enumerate(marks):
                for z in range(depth):
                    tile = jnp.where(lane == i * depth + z, mark[z * columns + y], tile)
            all_ref[which, y, depth * (width // STAT)] = tile.astype(BF)
    here = lax.axis_index("y")
    for k in range(columns):
        to = lax.rem(here + k, columns)
        refs[k][...] = all_ref[0, to]
        refs[columns + k][...] = all_ref[1, to]


def merge_tiles(parts):
    count = parts[0].shape[0] - 1
    groups = 8
    marks = [p[count].astype(F32) for p in parts]
    top = marks[0]
    for mark in marks[1:]:
        top = jnp.maximum(top, mark)
    scales = [jnp.exp(mark - top) for mark in marks]
    total = 0.0
    for scale, mark in zip(scales, marks):
        total += scale * (pltpu.roll(mark, STAT - groups, 1) + pltpu.roll(mark, STAT - 2 * groups, 1))
    size = count // groups
    bodies = []
    for z in range(groups):
        body = 0.0
        for scale, part in zip(scales, parts):
            body += scale[:, z:z + 1][None] * part[z * size:(z + 1) * size].astype(F32)
        bodies.append(body.astype(BF))
    high, low = split(total)
    return bodies, top, high, low


def merge_cores(a_ref, b_ref, out_ref):
    bodies, top, high, low = merge_tiles([a_ref, b_ref])
    size = bodies[0].shape[0]
    for z, body in enumerate(bodies):
        out_ref[z * size:(z + 1) * size] = body
    lane = iota(top.shape, 1)
    mark = jnp.where(lane < 16, pltpu.roll(high, 8, 1), jnp.where(lane < 24, pltpu.roll(low, 16, 1), 0.0))
    out_ref[len(bodies) * size] = jnp.where(lane < 8, top, mark).astype(BF)


def merge_columns(a_ref, b_ref, c_ref, d_ref, after_ref, out_ref):
    del after_ref
    bodies, top, high, low = merge_tiles([a_ref, b_ref, c_ref, d_ref])
    size = bodies[0].shape[0]
    lane = iota(top.shape, 1)
    for z, body in enumerate(bodies):
        out_ref[z, :size] = body
        out_ref[z, size] = stats(lane, top[:, z:z + 1], high[:, z:z + 1], low[:, z:z + 1]).astype(BF)


def merge_shards(in_ref, pay_ref, full_ref, side_ref):
    size = in_ref.shape[1] - 1
    marks = [in_ref[i, size].astype(F32) for i in range(in_ref.shape[0])]
    top = marks[0][:, 0:1]
    for mark in marks[1:]:
        top = jnp.maximum(top, mark[:, 0:1])
    acc, total = 0.0, 0.0
    for i, mark in enumerate(marks):
        scale = jnp.exp(mark[:, 0:1] - top)
        acc += scale[None] * in_ref[i, :size].astype(F32)
        total += scale * (mark[:, 1:2] + mark[:, 2:3])
    slots = total.shape[0] // 2
    first = iota((2 * slots, 1), 0) < slots
    full = acc / jnp.where(first, total, 1.0)[None]
    for j in range(size):
        full_ref[:, j * STAT:(j + 1) * STAT] = full[j]
        pay_ref[:, j * STAT:(j + 1) * STAT] = full[j].astype(BF)
    both = jnp.concatenate([total[:slots], total[:slots]], axis=0)
    side_ref[...] = jnp.where(iota((2 * slots, STAT), 1) == 0, top, both)


def gelu_parts(u):
    cdf = 0.5 * (1.0 + lax.erf(u * 0.7071067811865476))
    pdf = 0.3989422804014327 * jnp.exp(-0.5 * u * u)
    return u * cdf, cdf + u * pdf


def turn_weights(win_ref, wout_ref, after_ref, win_t_ref, wout_t_ref):
    del after_ref
    for e in range(win_ref.shape[0]):
        win_t_ref[e] = win_ref[e].T
        wout_t_ref[e] = wout_ref[e].T


def experts(own_ref, a_ref, b_ref, c_ref, win_ref, wout_ref, win_t_ref, wout_t_ref, *out_refs):
    blocks = [r[...].astype(F32) for r in (own_ref, a_ref, b_ref, c_ref)]
    fwd = jnp.concatenate([x[:4] for x in blocks], axis=0).astype(BF)
    bwd = jnp.concatenate([x[4:] for x in blocks], axis=0).astype(BF)
    rows = fwd.shape[0]
    out, back = 0.0, 0.0
    for e in range(win_ref.shape[0]):
        mine = (iota((rows, 1), 0) % 4) // 2 == e
        w1, w2 = win_ref[e], wout_ref[e]
        gelu, slope = gelu_parts(dot(fwd, w1))
        out += dot(jnp.where(mine, gelu, 0.0).astype(BF), w2)
        dact = dot(bwd, wout_t_ref[e])
        back += dot(jnp.where(mine, dact * slope, 0.0).astype(BF), win_t_ref[e])
    for v, ref in enumerate(out_refs):
        ref[...] = jnp.concatenate([out[4 * v:4 * v + 4], back[4 * v:4 * v + 4]], axis=0).astype(BF)


def finish_slots(own_ref, a_ref, b_ref, c_ref, full_ref, side_ref, out_ref):
    own, a, b, c = [r[...].astype(F32) for r in (own_ref, a_ref, b_ref, c_ref)]
    value = (own + a) + (b + c)
    width = value.shape[1]
    slots = value.shape[0] // 2
    first = iota((2 * slots, 1), 0) < slots
    side = side_ref[...]
    body = jnp.where(first, value, value / side[:, 1:2]).astype(BF)
    wide = body.astype(F32)
    shift = jnp.sum(full_ref[:slots, :] * wide[slots:, :], axis=1, keepdims=True)
    shift = jnp.concatenate([shift, shift], axis=0)
    high, low = split(shift)
    st = stats(iota((2 * slots, STAT), 1), side[:, 0:1], high, low).astype(BF)
    block = jnp.concatenate([body, st], axis=1)
    out_ref[...] = jnp.broadcast_to(block[None], out_ref.shape)


def token_grads(logit_ref, tok_ref, cot_ref, own_ref, oth_ref, *refs):
    *out_refs, dlog_ref, dexp_ref, comb_ref, so_ref, sc_ref, all_ref = refs
    core = lax.axis_index("c")
    logits, tok = logit_ref[...], tok_ref[...]
    n = logits.shape[1]
    width = tok.shape[1]
    zero = core == 0
    upper = iota((1, 8, 1), 1) < 4
    own, oth = own_ref[...].astype(F32), oth_ref[...].astype(F32)
    even, odd = jnp.where(zero, own, oth), jnp.where(zero, oth, own)
    first = jnp.where(upper, even, swap_halves(odd)).reshape(n, width + STAT)
    second = jnp.where(upper, swap_halves(even), odd).reshape(n, width + STAT)
    slot_out, scaled = first[:, :width].astype(BF), second[:, :width].astype(BF)
    so_ref[...] = slot_out
    sc_ref[...] = scaled
    side = first[:, width:].T
    point, shift = side[0:1, :], side[1:2, :] + side[2:3, :]
    comb = softmax_rows(logits)
    comb_ref[...] = comb.astype(BF)
    dexp = jnp.exp(logits - point).astype(BF)
    dexp_ref[...] = dexp
    dcomb = dot(cot_ref[...], slot_out, ((1,), (1,)))
    inner = dot(tok, scaled, ((1,), (1,)))
    dlog = comb * (dcomb - jnp.sum(comb * dcomb, axis=1, keepdims=True))
    dlog = (dlog + dexp.astype(F32) * (inner - shift)).astype(BF)
    dlog_ref[...] = dlog
    gp = dot(tok, dlog, ((0,), (0,))).reshape(width // 8, 8, n)
    left, right = gp[:, :, :n // 2], gp[:, :, n // 2:]
    even = jnp.where(upper, left, swap_halves(right)).astype(BF)
    odd = jnp.where(upper, swap_halves(left), right).astype(BF)
    all_ref[0] = jnp.where(zero, even, odd).reshape(all_ref.shape[1:])
    all_ref[1] = jnp.where(zero, odd, even).reshape(all_ref.shape[1:])
    here, steps = lax.axis_index("x"), all_ref.shape[1]
    for k in range(steps):
        to = lax.rem(here + k, steps)
        out_refs[k][...] = all_ref[0, to]
        out_refs[steps + k][...] = all_ref[1, to]


def token_outputs(comb_ref, so_ref, dlog_ref, par_ref, dexp_ref, sc_ref, mixed_ref, grad_ref):
    mixed_ref[...] = dot(comb_ref[...], so_ref[...]).astype(BF)
    grad = dot(dlog_ref[...], par_ref[...], ((1,), (1,)))
    grad_ref[...] = (grad + dot(dexp_ref[...], sc_ref[...])).astype(BF)


def add_halves(a_ref, b_ref, out_ref):
    out_ref[...] = (a_ref[...].astype(F32) + b_ref[...].astype(F32)).astype(BF)


def add_rows(own_ref, a_ref, b_ref, c_ref, after_ref, out_ref):
    del after_ref
    pairs = [r[...].astype(F32) for r in (own_ref, a_ref, b_ref, c_ref)]
    out_ref[...] = ((pairs[0] + pairs[1]) + (pairs[2] + pairs[3])).astype(BF)


def sum_pieces(in_ref, out_ref):
    value = in_ref[...].astype(F32)
    count, rows, half = value.shape
    total = jnp.sum(jnp.sum(value.reshape(count // 8, 8, rows, half), axis=0), axis=0)
    out_ref[:, :half] = total[:4]
    out_ref[:, half:] = total[4:]


def shifted(value, step, size, axis="x"):
    return lax.ppermute(value, axis, [(i, (i + step) % size) for i in range(size)])


def on_device(tokens, slot_parameters, w_in, w_out, grad_out):
    shape = jax.ShapeDtypeStruct
    tok, cot = tokens[0], grad_out[0]
    count, width = tok.shape
    n = slot_parameters.shape[1]
    videos = lax.axis_size("x")
    depth, rows_y = lax.axis_size("z"), lax.axis_size("y")
    owners = depth * rows_y
    wide = width + STAT
    unit = 2 * count * width * n
    swap = [(0, 1), (1, 0)]

    vmem = pl.BlockSpec(memory_space=pltpu.VMEM)
    tiles = (depth * (width // STAT) + 1, 8, STAT)
    *blocks, logits = pl.pallas_call(
        reduce_tokens,
        out_shape=[shape(tiles, BF)] * (2 * rows_y) + [shape((count, n), F32)],
        in_specs=[pl.BlockSpec(memory_space=pltpu.HBM)] * 3,
        out_specs=[vmem] * (2 * rows_y + 1),
        scratch_shapes=[
            pltpu.VMEM((count, width), BF), pltpu.VMEM((count, width), BF),
            pltpu.VMEM((width, n), BF), pltpu.VMEM((count, n), BF),
            pltpu.VMEM((2, rows_y) + tiles, BF),
            pltpu.SemaphoreType.DMA((PARTS + 2,)),
        ],
        compiler_params=PARAMS,
        cost_estimate=pl.CostEstimate(flops=4 * unit, bytes_accessed=4 << 20, transcendentals=0),
    )(*[pltpu.with_memory_space_constraint(a, pltpu.HBM) for a in (tok, cot, slot_parameters)])
    order = sorted(range(rows_y), key=lambda k: -min(k, rows_y - k))
    others = {k: lax.ppermute(blocks[rows_y + k], "c", swap) for k in order}
    shares = {}
    for k in order:
        (share,) = call(merge_cores, [shape(tiles, BF)], blocks[k], others[k], flops=10 * unit)
        if k:
            last = share
        shares[k] = shifted(share, k, rows_y, "y") if k else share
    win_t, wout_t = pl.pallas_call(
        turn_weights,
        out_shape=[shape(w_in.shape, BF), shape(w_out.shape, BF)],
        in_specs=[vmem, vmem, pl.BlockSpec(memory_space=pl.ANY)],
        out_specs=[vmem, vmem],
        compiler_params=PARAMS,
        cost_estimate=pl.CostEstimate(flops=20 * unit, bytes_accessed=8 * w_in.size, transcendentals=0),
    )(w_in, w_out, last)
    merged = pl.pallas_call(
        merge_columns,
        out_shape=shape((depth, width // STAT + 1, 8, STAT), BF),
        in_specs=[vmem] * rows_y + [pl.BlockSpec(memory_space=pl.ANY)],
        out_specs=vmem,
        compiler_params=PARAMS,
    )(*[shares[k] for k in range(rows_y)], wout_t)
    shards = lax.all_to_all(merged, "z", 0, 0, tiled=True)
    pay, full, side = call(
        merge_shards,
        [shape((8, width), BF), shape((8, width), F32), shape((8, STAT), F32)],
        shards,
    )
    behind = [shifted(pay, k, videos) for k in range(1, videos)]
    partial = call(
        experts, [shape((8, width), BF)] * videos, pay, *behind, w_in, w_out, win_t, wout_t,
        flops=32 * videos * w_in.size,
    )
    parts = [shifted(partial[k], -k, videos) for k in range(1, videos)]
    (block,) = call(finish_slots, [shape((owners, 8, wide), BF)], partial[0], *parts, full, side)
    mine = lax.all_to_all(block, ZY, 0, 0, tiled=True)
    theirs = lax.ppermute(mine, "c", swap)

    quarter = shape((owners, 8, n // 2), BF)
    *quarters, dlog, dexp, comb, slot_out, scaled = call(
        token_grads,
        [quarter] * (2 * videos)
        + [shape((count, n), BF), shape((count, n), BF), shape((count, n), BF),
           shape((n, width), BF), shape((n, width), BF)],
        logits, tok, cot, mine, theirs, flops=5 * unit,
        scratch=[pltpu.VMEM((2, videos) + quarter.shape, BF)],
    )
    order = sorted(range(videos), key=lambda k: -min(k, videos - k))
    others = {k: lax.ppermute(quarters[videos + k], "c", swap) for k in order}
    shares = {}
    for k in order:
        (share,) = call(add_halves, [quarter], quarters[k], others[k])
        shares[k] = shifted(share, k, videos) if k else share
    mixed, grad_tokens = call(
        token_outputs,
        [shape((count, width), BF), shape((count, width), BF)],
        comb, slot_out, dlog, slot_parameters, dexp, scaled, flops=3 * unit,
    )
    half = pl.pallas_call(
        add_rows,
        out_shape=quarter,
        in_specs=[vmem] * videos + [pl.BlockSpec(memory_space=pltpu.HBM)],
        out_specs=vmem,
        compiler_params=PARAMS,
    )(*[shares[k] for k in range(videos)], pltpu.with_memory_space_constraint(mixed, pltpu.HBM))
    pieces = lax.all_to_all(half, ZY, 0, 0, tiled=True)
    (grad_params,) = call(sum_pieces, [shape((4, n), F32)], pieces)
    return mixed[None], grad_tokens[None], grad_params


def solution(mesh):
    sizes = dict(mesh.shape)
    grid = Mesh(mesh.devices.reshape(sizes["batch"], sizes["seq"] // 8, 4, 2), AXES)
    seq = ("z", "y", "c")
    placed = (
        P("x", seq, None),
        P(),
        P(seq, None, "x"),
        P(seq, "x", None),
        P("x", seq, None),
    )
    return jax.shard_map(
        on_device,
        mesh=grid,
        in_specs=placed,
        out_specs=(P("x", seq, None), P("x", seq, None), P(AXES, None)),
        check_vma=False,
    )
```

```python
import math

import jax
import jax.numpy as jnp
from jax import lax
from jax.experimental import pallas as pl
from jax.experimental.pallas import tpu as pltpu
from jax.sharding import Mesh, PartitionSpec as P

BF = jnp.bfloat16
F32 = jnp.float32
AXES = ("x", "z", "y", "c")
ZY = ("z", "y")
PARTS = 2
STAT = 128
PARAMS = pltpu.CompilerParams(vmem_limit_bytes=24 * 1024 * 1024)


def dot(a, b, contract=((1,), (0,))):
    return lax.dot_general(a, b, (contract, ((), ())), preferred_element_type=F32)


def iota(shape, dim):
    return lax.broadcasted_iota(jnp.int32, shape, dim)


def call(body, outs, *args, flops=0, scratch=(), params=PARAMS):
    nbytes = sum(a.size * a.dtype.itemsize for a in args)
    nbytes += sum(math.prod(o.shape) * 4 for o in outs)
    return pl.pallas_call(
        body,
        out_shape=outs,
        in_specs=[pl.BlockSpec(memory_space=pltpu.VMEM)] * len(args),
        out_specs=[pl.BlockSpec(memory_space=pltpu.VMEM)] * len(outs),
        scratch_shapes=list(scratch),
        compiler_params=params,
        cost_estimate=pl.CostEstimate(flops=flops, bytes_accessed=nbytes, transcendentals=0),
    )(*args)


def split(value):
    high = value.astype(BF).astype(F32)
    return high, (value - high).astype(BF).astype(F32)


def stats(lane, first, second, third):
    return jnp.where(lane == 0, first, jnp.where(lane == 1, second, jnp.where(lane == 2, third, 0.0)))


def softmax_rows(logits):
    e = jnp.exp(logits - jnp.max(logits, axis=1, keepdims=True))
    return e / jnp.sum(e, axis=1, keepdims=True)


def swap_halves(value):
    return pltpu.roll(value, 4, 1)


def reduce_tokens(tok_hbm, cot_hbm, par_hbm, *refs):
    *refs, logit_ref, tok_ref, cot_ref, par_ref, comb_ref, all_ref, sems = refs
    core = lax.axis_index("c")
    count, width = tok_ref.shape
    n = par_ref.shape[1]
    part = count // PARTS
    copies = [pltpu.make_async_copy(par_hbm, par_ref, sems.at[0])]
    for i in range(PARTS):
        rows = pl.ds(i * part, part)
        copies.append(pltpu.make_async_copy(tok_hbm.at[rows], tok_ref.at[rows], sems.at[1 + i]))
    copies.append(pltpu.make_async_copy(cot_hbm, cot_ref, sems.at[1 + PARTS]))
    for copy in copies:
        copy.start()
    copies[0].wait()
    par = par_ref[...]
    peak = None
    for i in range(PARTS):
        rows = pl.ds(i * part, part)
        copies[1 + i].wait()
        piece = dot(tok_ref[rows, :], par)
        logit_ref[rows, :] = piece
        comb_ref[rows, :] = softmax_rows(piece).astype(BF)
        high = jnp.max(piece, axis=0, keepdims=True)
        peak = high if peak is None else jnp.maximum(peak, high)
    refpoint = peak.astype(BF).astype(F32)
    dexp = jnp.exp(logit_ref[...] - refpoint).astype(BF)
    numer = dot(dexp, tok_ref[...], ((0,), (0,))).reshape(n // 8, 8, width)
    total = dot(dexp, jnp.ones((count, STAT), BF), ((0,), (0,)))
    diag = jnp.where(iota((n, n), 0) == iota((n, n), 1), refpoint, 0.0).astype(BF)
    point = dot(diag, jnp.ones((n, STAT), BF))
    high, low = split(total)
    copies[1 + PARTS].wait()
    dslot = dot(comb_ref[...], cot_ref[...], ((0,), (0,))).reshape(n // 8, 8, width)
    upper = iota((1, 8, 1), 1) < 4
    zero = core == 0
    even = jnp.where(upper, numer, swap_halves(dslot)).astype(BF)
    odd = jnp.where(upper, swap_halves(numer), dslot).astype(BF)
    sides = [value.reshape(n // 8, 8, STAT) for value in (point, high, low)]
    even_sides = [jnp.where(upper, value, 0.0) for value in sides]
    odd_sides = [jnp.where(upper, swap_halves(value), 0.0) for value in sides]
    columns = all_ref.shape[1]
    depth = n // 8 // columns
    keep = jnp.where(zero, even, odd)
    send = jnp.where(zero, odd, even)
    keep_sides = [jnp.where(zero, e, o) for e, o in zip(even_sides, odd_sides)]
    send_sides = [jnp.where(zero, o, e) for e, o in zip(even_sides, odd_sides)]
    lane = iota((8, STAT), 1)
    for which, (value, marks) in enumerate(((keep, keep_sides), (send, send_sides))):
        for y in range(columns):
            for z in range(depth):
                for j in range(width // STAT):
                    all_ref[which, y, z * (width // STAT) + j] = value[z * columns + y, :, j * STAT:(j + 1) * STAT]
            tile = jnp.zeros((8, STAT), F32)
            for i, mark in enumerate(marks):
                for z in range(depth):
                    tile = jnp.where(lane == i * depth + z, mark[z * columns + y], tile)
            all_ref[which, y, depth * (width // STAT)] = tile.astype(BF)
    here = lax.axis_index("y")
    for k in range(columns):
        to = lax.rem(here + k, columns)
        refs[k][...] = all_ref[0, to]
        refs[columns + k][...] = all_ref[1, to]


def merge_tiles(parts):
    count = parts[0].shape[0] - 1
    groups = 8
    marks = [p[count].astype(F32) for p in parts]
    top = marks[0]
    for mark in marks[1:]:
        top = jnp.maximum(top, mark)
    scales = [jnp.exp(mark - top) for mark in marks]
    total = 0.0
    for scale, mark in zip(scales, marks):
        total += scale * (pltpu.roll(mark, STAT - groups, 1) + pltpu.roll(mark, STAT - 2 * groups, 1))
    size = count // groups
    bodies = []
    for z in range(groups):
        body = 0.0
        for scale, part in zip(scales, parts):
            body += scale[:, z:z + 1][None] * part[z * size:(z + 1) * size].astype(F32)
        bodies.append(body.astype(BF))
    high, low = split(total)
    return bodies, top, high, low


def merge_cores(a_ref, b_ref, out_ref):
    bodies, top, high, low = merge_tiles([a_ref, b_ref])
    size = bodies[0].shape[0]
    for z, body in enumerate(bodies):
        out_ref[z * size:(z + 1) * size] = body
    lane = iota(top.shape, 1)
    mark = jnp.where(lane < 16, pltpu.roll(high, 8, 1), jnp.where(lane < 24, pltpu.roll(low, 16, 1), 0.0))
    out_ref[len(bodies) * size] = jnp.where(lane < 8, top, mark).astype(BF)


def merge_columns(a_ref, b_ref, c_ref, d_ref, after_ref, out_ref):
    del after_ref
    bodies, top, high, low = merge_tiles([a_ref, b_ref, c_ref, d_ref])
    size = bodies[0].shape[0]
    lane = iota(top.shape, 1)
    for z, body in enumerate(bodies):
        out_ref[z, :size] = body
        out_ref[z, size] = stats(lane, top[:, z:z + 1], high[:, z:z + 1], low[:, z:z + 1]).astype(BF)


def merge_shards(in_ref, pay_ref, full_ref, side_ref):
    size = in_ref.shape[1] - 1
    marks = [in_ref[i, size].astype(F32) for i in range(in_ref.shape[0])]
    top = marks[0][:, 0:1]
    for mark in marks[1:]:
        top = jnp.maximum(top, mark[:, 0:1])
    acc, total = 0.0, 0.0
    for i, mark in enumerate(marks):
        scale = jnp.exp(mark[:, 0:1] - top)
        acc += scale[None] * in_ref[i, :size].astype(F32)
        total += scale * (mark[:, 1:2] + mark[:, 2:3])
    slots = total.shape[0] // 2
    first = iota((2 * slots, 1), 0) < slots
    full = acc / jnp.where(first, total, 1.0)[None]
    for j in range(size):
        full_ref[:, j * STAT:(j + 1) * STAT] = full[j]
        pay_ref[:, j * STAT:(j + 1) * STAT] = full[j].astype(BF)
    both = jnp.concatenate([total[:slots], total[:slots]], axis=0)
    side_ref[...] = jnp.where(iota((2 * slots, STAT), 1) == 0, top, both)


def gelu_parts(u):
    cdf = 0.5 * (1.0 + lax.erf(u * 0.7071067811865476))
    pdf = 0.3989422804014327 * jnp.exp(-0.5 * u * u)
    return u * cdf, cdf + u * pdf


def turn_weights(win_ref, wout_ref, after_ref, win_t_ref, wout_t_ref):
    del after_ref
    for e in range(win_ref.shape[0]):
        win_t_ref[e] = win_ref[e].T
        wout_t_ref[e] = wout_ref[e].T


def experts(own_ref, a_ref, b_ref, c_ref, win_ref, wout_ref, win_t_ref, wout_t_ref, *out_refs):
    blocks = [r[...].astype(F32) for r in (own_ref, a_ref, b_ref, c_ref)]
    fwd = jnp.concatenate([x[:4] for x in blocks], axis=0).astype(BF)
    bwd = jnp.concatenate([x[4:] for x in blocks], axis=0).astype(BF)
    rows = fwd.shape[0]
    out, back = 0.0, 0.0
    for e in range(win_ref.shape[0]):
        mine = (iota((rows, 1), 0) % 4) // 2 == e
        w1, w2 = win_ref[e], wout_ref[e]
        gelu, slope = gelu_parts(dot(fwd, w1))
        out += dot(jnp.where(mine, gelu, 0.0).astype(BF), w2)
        dact = dot(bwd, wout_t_ref[e])
        back += dot(jnp.where(mine, dact * slope, 0.0).astype(BF), win_t_ref[e])
    for v, ref in enumerate(out_refs):
        ref[...] = jnp.concatenate([out[4 * v:4 * v + 4], back[4 * v:4 * v + 4]], axis=0).astype(BF)


def finish_slots(own_ref, a_ref, b_ref, c_ref, full_ref, side_ref, out_ref):
    own, a, b, c = [r[...].astype(F32) for r in (own_ref, a_ref, b_ref, c_ref)]
    value = (own + a) + (b + c)
    width = value.shape[1]
    slots = value.shape[0] // 2
    first = iota((2 * slots, 1), 0) < slots
    side = side_ref[...]
    body = jnp.where(first, value, value / side[:, 1:2]).astype(BF)
    wide = body.astype(F32)
    shift = jnp.sum(full_ref[:slots, :] * wide[slots:, :], axis=1, keepdims=True)
    shift = jnp.concatenate([shift, shift], axis=0)
    high, low = split(shift)
    st = stats(iota((2 * slots, STAT), 1), side[:, 0:1], high, low)
    block = jnp.concatenate([wide[:slots], pltpu.roll(wide, slots, 0)[:slots], st[:slots]], axis=1).astype(BF)
    out_ref[...] = jnp.broadcast_to(block[None], out_ref.shape)


def token_grads(logit_ref, tok_ref, cot_ref, own_ref, oth_ref, *refs):
    *out_refs, dlog_ref, dexp_ref, comb_ref, so_ref, sc_ref, all_ref = refs
    core = lax.axis_index("c")
    logits, tok = logit_ref[...], tok_ref[...]
    n = logits.shape[1]
    width = tok.shape[1]
    zero = core == 0
    upper = iota((1, 8, 1), 1) < 4
    own, oth = own_ref[...].astype(F32), oth_ref[...].astype(F32)
    even, odd = jnp.where(zero, own, oth), jnp.where(zero, oth, own)
    both = jnp.concatenate([even, odd], axis=1).reshape(n, 2 * width + STAT)
    slot_out, scaled = both[:, :width].astype(BF), both[:, width:2 * width].astype(BF)
    so_ref[...] = slot_out
    sc_ref[...] = scaled
    side = both[:, 2 * width:].T
    point, shift = side[0:1, :], side[1:2, :] + side[2:3, :]
    comb = softmax_rows(logits)
    comb_ref[...] = comb.astype(BF)
    dexp = jnp.exp(logits - point).astype(BF)
    dexp_ref[...] = dexp
    dcomb = dot(cot_ref[...], slot_out, ((1,), (1,)))
    inner = dot(tok, scaled, ((1,), (1,)))
    dlog = comb * (dcomb - jnp.sum(comb * dcomb, axis=1, keepdims=True))
    dlog = (dlog + dexp.astype(F32) * (inner - shift)).astype(BF)
    dlog_ref[...] = dlog
    gp = dot(tok, dlog, ((0,), (0,))).reshape(width // 8, 8, n)
    left, right = gp[:, :, :n // 2], gp[:, :, n // 2:]
    even = jnp.where(upper, left, swap_halves(right)).astype(BF)
    odd = jnp.where(upper, swap_halves(left), right).astype(BF)
    all_ref[0] = jnp.where(zero, even, odd).reshape(all_ref.shape[1:])
    all_ref[1] = jnp.where(zero, odd, even).reshape(all_ref.shape[1:])
    here, steps = lax.axis_index("x"), all_ref.shape[1]
    for k in range(steps):
        to = lax.rem(here + k, steps)
        out_refs[k][...] = all_ref[0, to]
        out_refs[steps + k][...] = all_ref[1, to]


def token_outputs(comb_ref, so_ref, dlog_ref, par_ref, dexp_ref, sc_ref, mixed_ref, grad_ref):
    mixed_ref[...] = dot(comb_ref[...], so_ref[...]).astype(BF)
    grad = dot(dlog_ref[...], par_ref[...], ((1,), (1,)))
    grad_ref[...] = (grad + dot(dexp_ref[...], sc_ref[...])).astype(BF)


def add_halves(a_ref, b_ref, out_ref):
    out_ref[...] = (a_ref[...].astype(F32) + b_ref[...].astype(F32)).astype(BF)


def add_rows(own_ref, a_ref, b_ref, c_ref, after_ref, out_ref):
    del after_ref
    pairs = [r[...].astype(F32) for r in (own_ref, a_ref, b_ref, c_ref)]
    out_ref[...] = ((pairs[0] + pairs[1]) + (pairs[2] + pairs[3])).astype(BF)


def sum_pieces(in_ref, out_ref):
    value = in_ref[...].astype(F32)
    count, rows, half = value.shape
    total = jnp.sum(jnp.sum(value.reshape(count // 8, 8, rows, half), axis=0), axis=0)
    out_ref[:, :half] = total[:4]
    out_ref[:, half:] = total[4:]


def shifted(value, step, size, axis="x"):
    return lax.ppermute(value, axis, [(i, (i + step) % size) for i in range(size)])


def on_device(tokens, slot_parameters, w_in, w_out, grad_out):
    shape = jax.ShapeDtypeStruct
    tok, cot = tokens[0], grad_out[0]
    count, width = tok.shape
    n = slot_parameters.shape[1]
    videos = lax.axis_size("x")
    depth, rows_y = lax.axis_size("z"), lax.axis_size("y")
    owners = depth * rows_y
    wide = width + STAT
    unit = 2 * count * width * n
    swap = [(0, 1), (1, 0)]

    vmem = pl.BlockSpec(memory_space=pltpu.VMEM)
    tiles = (depth * (width // STAT) + 1, 8, STAT)
    *blocks, logits = pl.pallas_call(
        reduce_tokens,
        out_shape=[shape(tiles, BF)] * (2 * rows_y) + [shape((count, n), F32)],
        in_specs=[pl.BlockSpec(memory_space=pltpu.HBM)] * 3,
        out_specs=[vmem] * (2 * rows_y + 1),
        scratch_shapes=[
            pltpu.VMEM((count, width), BF), pltpu.VMEM((count, width), BF),
            pltpu.VMEM((width, n), BF), pltpu.VMEM((count, n), BF),
            pltpu.VMEM((2, rows_y) + tiles, BF),
            pltpu.SemaphoreType.DMA((PARTS + 2,)),
        ],
        compiler_params=PARAMS,
        cost_estimate=pl.CostEstimate(flops=4 * unit, bytes_accessed=4 << 20, transcendentals=0),
    )(*[pltpu.with_memory_space_constraint(a, pltpu.HBM) for a in (tok, cot, slot_parameters)])
    order = sorted(range(rows_y), key=lambda k: -min(k, rows_y - k))
    others = {k: lax.ppermute(blocks[rows_y + k], "c", swap) for k in order}
    shares = {}
    for k in order:
        (share,) = call(merge_cores, [shape(tiles, BF)], blocks[k], others[k], flops=10 * unit)
        if k:
            last = share
        shares[k] = shifted(share, k, rows_y, "y") if k else share
    win_t, wout_t = pl.pallas_call(
        turn_weights,
        out_shape=[shape(w_in.shape, BF), shape(w_out.shape, BF)],
        in_specs=[vmem, vmem, pl.BlockSpec(memory_space=pl.ANY)],
        out_specs=[vmem, vmem],
        compiler_params=PARAMS,
        cost_estimate=pl.CostEstimate(flops=20 * unit, bytes_accessed=8 * w_in.size, transcendentals=0),
    )(w_in, w_out, last)
    merged = pl.pallas_call(
        merge_columns,
        out_shape=shape((depth, width // STAT + 1, 8, STAT), BF),
        in_specs=[vmem] * rows_y + [pl.BlockSpec(memory_space=pl.ANY)],
        out_specs=vmem,
        compiler_params=PARAMS,
    )(*[shares[k] for k in range(rows_y)], wout_t)
    shards = lax.all_to_all(merged, "z", 0, 0, tiled=True)
    pay, full, side = call(
        merge_shards,
        [shape((8, width), BF), shape((8, width), F32), shape((8, STAT), F32)],
        shards,
    )
    behind = [shifted(pay, k, videos) for k in range(1, videos)]
    partial = call(
        experts, [shape((8, width), BF)] * videos, pay, *behind, w_in, w_out, win_t, wout_t,
        flops=32 * videos * w_in.size,
    )
    parts = [shifted(partial[k], -k, videos) for k in range(1, videos)]
    (block,) = call(finish_slots, [shape((owners, 4, 2 * width + STAT), BF)], partial[0], *parts, full, side)
    mine = lax.all_to_all(block, ZY, 0, 0, tiled=True)
    theirs = lax.ppermute(mine, "c", swap)

    quarter = shape((owners, 8, n // 2), BF)
    *quarters, dlog, dexp, comb, slot_out, scaled = call(
        token_grads,
        [quarter] * (2 * videos)
        + [shape((count, n), BF), shape((count, n), BF), shape((count, n), BF),
           shape((n, width), BF), shape((n, width), BF)],
        logits, tok, cot, mine, theirs, flops=5 * unit,
        scratch=[pltpu.VMEM((2, videos) + quarter.shape, BF)],
    )
    order = sorted(range(videos), key=lambda k: -min(k, videos - k))
    others = {k: lax.ppermute(quarters[videos + k], "c", swap) for k in order}
    shares = {}
    for k in order:
        (share,) = call(add_halves, [quarter], quarters[k], others[k])
        shares[k] = shifted(share, k, videos) if k else share
    mixed, grad_tokens = call(
        token_outputs,
        [shape((count, width), BF), shape((count, width), BF)],
        comb, slot_out, dlog, slot_parameters, dexp, scaled, flops=3 * unit,
    )
    half = pl.pallas_call(
        add_rows,
        out_shape=quarter,
        in_specs=[vmem] * videos + [pl.BlockSpec(memory_space=pltpu.HBM)],
        out_specs=vmem,
        compiler_params=PARAMS,
    )(*[shares[k] for k in range(videos)], pltpu.with_memory_space_constraint(mixed, pltpu.HBM))
    pieces = lax.all_to_all(half, ZY, 0, 0, tiled=True)
    (grad_params,) = call(sum_pieces, [shape((4, n), F32)], pieces)
    return mixed[None], grad_tokens[None], grad_params


def solution(mesh):
    sizes = dict(mesh.shape)
    grid = Mesh(mesh.devices.reshape(sizes["batch"], sizes["seq"] // 8, 4, 2), AXES)
    seq = ("z", "y", "c")
    placed = (
        P("x", seq, None),
        P(),
        P(seq, None, "x"),
        P(seq, "x", None),
        P("x", seq, None),
    )
    return jax.shard_map(
        on_device,
        mesh=grid,
        in_specs=placed,
        out_specs=(P("x", seq, None), P("x", seq, None), P(AXES, None)),
        check_vma=False,
    )
```

```python
import math

import jax
import jax.numpy as jnp
from jax import lax
from jax.experimental import pallas as pl
from jax.experimental.pallas import tpu as pltpu
from jax.sharding import Mesh, PartitionSpec as P

BF = jnp.bfloat16
F32 = jnp.float32
AXES = ("x", "z", "y", "c")
ZY = ("z", "y")
PARTS = 2
STAT = 128
PARAMS = pltpu.CompilerParams(vmem_limit_bytes=24 * 1024 * 1024)


def dot(a, b, contract=((1,), (0,))):
    return lax.dot_general(a, b, (contract, ((), ())), preferred_element_type=F32)


def iota(shape, dim):
    return lax.broadcasted_iota(jnp.int32, shape, dim)


def call(body, outs, *args, flops=0, scratch=(), params=PARAMS):
    nbytes = sum(a.size * a.dtype.itemsize for a in args)
    nbytes += sum(math.prod(o.shape) * 4 for o in outs)
    return pl.pallas_call(
        body,
        out_shape=outs,
        in_specs=[pl.BlockSpec(memory_space=pltpu.VMEM)] * len(args),
        out_specs=[pl.BlockSpec(memory_space=pltpu.VMEM)] * len(outs),
        scratch_shapes=list(scratch),
        compiler_params=params,
        cost_estimate=pl.CostEstimate(flops=flops, bytes_accessed=nbytes, transcendentals=0),
    )(*args)


def split(value):
    high = value.astype(BF).astype(F32)
    return high, (value - high).astype(BF).astype(F32)


def split3(value):
    high = value.astype(BF).astype(F32)
    return (high,) + split(value - high)


def stats(lane, *values):
    tile = jnp.zeros(lane.shape, F32)
    for i, value in enumerate(values):
        tile = jnp.where(lane == i, value, tile)
    return tile


def softmax_rows(logits):
    e = jnp.exp(logits - jnp.max(logits, axis=1, keepdims=True))
    return e / jnp.sum(e, axis=1, keepdims=True)


def swap_halves(value):
    return pltpu.roll(value, 4, 1)


def reduce_tokens(tok_hbm, cot_hbm, par_hbm, *refs):
    *refs, logit_ref, tok_ref, cot_ref, par_ref, comb_ref, all_ref, sems = refs
    core = lax.axis_index("c")
    count, width = tok_ref.shape
    n = par_ref.shape[1]
    part = count // PARTS
    copies = [pltpu.make_async_copy(par_hbm, par_ref, sems.at[0])]
    for i in range(PARTS):
        rows = pl.ds(i * part, part)
        copies.append(pltpu.make_async_copy(tok_hbm.at[rows], tok_ref.at[rows], sems.at[1 + i]))
    copies.append(pltpu.make_async_copy(cot_hbm, cot_ref, sems.at[1 + PARTS]))
    for copy in copies:
        copy.start()
    copies[0].wait()
    par = par_ref[...]
    peak = None
    for i in range(PARTS):
        rows = pl.ds(i * part, part)
        copies[1 + i].wait()
        piece = dot(tok_ref[rows, :], par)
        logit_ref[rows, :] = piece
        comb_ref[rows, :] = softmax_rows(piece).astype(BF)
        high = jnp.max(piece, axis=0, keepdims=True)
        peak = high if peak is None else jnp.maximum(peak, high)
    refpoint = peak
    dexp = jnp.exp(logit_ref[...] - refpoint).astype(BF)
    numer = dot(dexp, tok_ref[...], ((0,), (0,))).reshape(n // 8, 8, width)
    total = dot(dexp, jnp.ones((count, STAT), BF), ((0,), (0,)))
    same, ones = iota((n, n), 0) == iota((n, n), 1), jnp.ones((n, STAT), BF)
    point, middle, last = [dot(jnp.where(same, v, 0.0).astype(BF), ones) for v in split3(refpoint)]
    high, low = split(total)
    copies[1 + PARTS].wait()
    dslot = dot(comb_ref[...], cot_ref[...], ((0,), (0,))).reshape(n // 8, 8, width)
    upper = iota((1, 8, 1), 1) < 4
    zero = core == 0
    even = jnp.where(upper, numer, swap_halves(dslot)).astype(BF)
    odd = jnp.where(upper, swap_halves(numer), dslot).astype(BF)
    sides = [value.reshape(n // 8, 8, STAT) for value in (point, high, low, middle, last)]
    even_sides = [jnp.where(upper, value, 0.0) for value in sides]
    odd_sides = [jnp.where(upper, swap_halves(value), 0.0) for value in sides]
    columns = all_ref.shape[1]
    depth = n // 8 // columns
    keep = jnp.where(zero, even, odd)
    send = jnp.where(zero, odd, even)
    keep_sides = [jnp.where(zero, e, o) for e, o in zip(even_sides, odd_sides)]
    send_sides = [jnp.where(zero, o, e) for e, o in zip(even_sides, odd_sides)]
    lane = iota((8, STAT), 1)
    for which, (value, marks) in enumerate(((keep, keep_sides), (send, send_sides))):
        for y in range(columns):
            for z in range(depth):
                for j in range(width // STAT):
                    all_ref[which, y, z * (width // STAT) + j] = value[z * columns + y, :, j * STAT:(j + 1) * STAT]
            tile = jnp.zeros((8, STAT), F32)
            for i, mark in enumerate(marks):
                for z in range(depth):
                    tile = jnp.where(lane == i * depth + z, mark[z * columns + y], tile)
            all_ref[which, y, depth * (width // STAT)] = tile.astype(BF)
    here = lax.axis_index("y")
    for k in range(columns):
        to = lax.rem(here + k, columns)
        refs[k][...] = all_ref[0, to]
        refs[columns + k][...] = all_ref[1, to]


def merge_tiles(parts):
    count = parts[0].shape[0] - 1
    groups = 8
    marks = [p[count].astype(F32) for p in parts]
    points = [mark + pltpu.roll(mark, STAT - 3 * groups, 1) + pltpu.roll(mark, STAT - 4 * groups, 1) for mark in marks]
    top = points[0]
    for point in points[1:]:
        top = jnp.maximum(top, point)
    scales = [jnp.exp(point - top) for point in points]
    total = 0.0
    for scale, mark in zip(scales, marks):
        total += scale * (pltpu.roll(mark, STAT - groups, 1) + pltpu.roll(mark, STAT - 2 * groups, 1))
    size = count // groups
    bodies = []
    for z in range(groups):
        body = 0.0
        for scale, part in zip(scales, parts):
            body += scale[:, z:z + 1][None] * part[z * size:(z + 1) * size].astype(F32)
        bodies.append(body.astype(BF))
    high, low = split(total)
    return bodies, top, high, low


def merge_cores(a_ref, b_ref, out_ref):
    bodies, top, high, low = merge_tiles([a_ref, b_ref])
    size = bodies[0].shape[0]
    for z, body in enumerate(bodies):
        out_ref[z * size:(z + 1) * size] = body
    lane = iota(top.shape, 1)
    point, middle, last = split3(top)
    tile = jnp.zeros(top.shape, F32)
    for i, mark in enumerate((point, high, low, middle, last)):
        tile = jnp.where(lane // 8 == i, pltpu.roll(mark, 8 * i, 1) if i else mark, tile)
    out_ref[len(bodies) * size] = tile.astype(BF)


def merge_columns(a_ref, b_ref, c_ref, d_ref, after_ref, out_ref):
    del after_ref
    bodies, top, high, low = merge_tiles([a_ref, b_ref, c_ref, d_ref])
    size = bodies[0].shape[0]
    lane = iota(top.shape, 1)
    for z, body in enumerate(bodies):
        out_ref[z, :size] = body
        point, middle, last = split3(top[:, z:z + 1])
        out_ref[z, size] = stats(lane, point, high[:, z:z + 1], low[:, z:z + 1], middle, last).astype(BF)


def merge_shards(in_ref, pay_ref, full_ref, side_ref):
    size = in_ref.shape[1] - 1
    marks = [in_ref[i, size].astype(F32) for i in range(in_ref.shape[0])]
    points = [mark[:, 0:1] + mark[:, 3:4] + mark[:, 4:5] for mark in marks]
    top = points[0]
    for point in points[1:]:
        top = jnp.maximum(top, point)
    acc, total = 0.0, 0.0
    for i, mark in enumerate(marks):
        scale = jnp.exp(points[i] - top)
        acc += scale[None] * in_ref[i, :size].astype(F32)
        total += scale * (mark[:, 1:2] + mark[:, 2:3])
    slots = total.shape[0] // 2
    first = iota((2 * slots, 1), 0) < slots
    full = acc / jnp.where(first, total, 1.0)[None]
    for j in range(size):
        full_ref[:, j * STAT:(j + 1) * STAT] = full[j]
        pay_ref[:, j * STAT:(j + 1) * STAT] = full[j].astype(BF)
    both = jnp.concatenate([total[:slots], total[:slots]], axis=0)
    side_ref[...] = jnp.where(iota((2 * slots, STAT), 1) == 0, top, both)


def gelu_parts(u):
    cdf = 0.5 * (1.0 + lax.erf(u * 0.7071067811865476))
    pdf = 0.3989422804014327 * jnp.exp(-0.5 * u * u)
    return u * cdf, cdf + u * pdf


def turn_weights(win_ref, wout_ref, after_ref, win_t_ref, wout_t_ref):
    del after_ref
    for e in range(win_ref.shape[0]):
        win_t_ref[e] = win_ref[e].T
        wout_t_ref[e] = wout_ref[e].T


def experts(own_ref, a_ref, b_ref, c_ref, win_ref, wout_ref, win_t_ref, wout_t_ref, *out_refs):
    blocks = [r[...].astype(F32) for r in (own_ref, a_ref, b_ref, c_ref)]
    fwd = jnp.concatenate([x[:4] for x in blocks], axis=0).astype(BF)
    bwd = jnp.concatenate([x[4:] for x in blocks], axis=0).astype(BF)
    rows = fwd.shape[0]
    out, back = 0.0, 0.0
    for e in range(win_ref.shape[0]):
        mine = (iota((rows, 1), 0) % 4) // 2 == e
        w1, w2 = win_ref[e], wout_ref[e]
        gelu, slope = gelu_parts(dot(fwd, w1))
        out += dot(jnp.where(mine, gelu, 0.0).astype(BF), w2)
        dact = dot(bwd, wout_t_ref[e])
        back += dot(jnp.where(mine, dact * slope, 0.0).astype(BF), win_t_ref[e])
    for v, ref in enumerate(out_refs):
        ref[...] = jnp.concatenate([out[4 * v:4 * v + 4], back[4 * v:4 * v + 4]], axis=0).astype(BF)


def finish_slots(own_ref, a_ref, b_ref, c_ref, full_ref, side_ref, out_ref):
    own, a, b, c = [r[...].astype(F32) for r in (own_ref, a_ref, b_ref, c_ref)]
    value = (own + a) + (b + c)
    width = value.shape[1]
    slots = value.shape[0] // 2
    first = iota((2 * slots, 1), 0) < slots
    side = side_ref[...]
    body = jnp.where(first, value, value / side[:, 1:2]).astype(BF)
    wide = body.astype(F32)
    shift = jnp.sum(full_ref[:slots, :] * wide[slots:, :], axis=1, keepdims=True)
    shift = jnp.concatenate([shift, shift], axis=0)
    high, low = split(shift)
    point, middle, last = split3(side[:, 0:1])
    st = stats(iota((2 * slots, STAT), 1), point, high, low, middle, last)
    block = jnp.concatenate([wide[:slots], pltpu.roll(wide, slots, 0)[:slots], st[:slots]], axis=1).astype(BF)
    out_ref[...] = jnp.broadcast_to(block[None], out_ref.shape)


def token_grads(logit_ref, tok_ref, cot_ref, own_ref, oth_ref, *refs):
    *out_refs, dlog_ref, dexp_ref, comb_ref, so_ref, sc_ref, all_ref = refs
    core = lax.axis_index("c")
    logits, tok = logit_ref[...], tok_ref[...]
    n = logits.shape[1]
    width = tok.shape[1]
    zero = core == 0
    upper = iota((1, 8, 1), 1) < 4
    own, oth = own_ref[...].astype(F32), oth_ref[...].astype(F32)
    even, odd = jnp.where(zero, own, oth), jnp.where(zero, oth, own)
    both = jnp.concatenate([even, odd], axis=1).reshape(n, 2 * width + STAT)
    slot_out, scaled = both[:, :width].astype(BF), both[:, width:2 * width].astype(BF)
    so_ref[...] = slot_out
    sc_ref[...] = scaled
    side = both[:, 2 * width:].T
    point, shift = side[0:1, :] + side[3:4, :] + side[4:5, :], side[1:2, :] + side[2:3, :]
    comb = softmax_rows(logits)
    comb_ref[...] = comb.astype(BF)
    dexp = jnp.exp(logits - point).astype(BF)
    dexp_ref[...] = dexp
    dcomb = dot(cot_ref[...], slot_out, ((1,), (1,)))
    inner = dot(tok, scaled, ((1,), (1,)))
    dlog = comb * (dcomb - jnp.sum(comb * dcomb, axis=1, keepdims=True))
    dlog = (dlog + dexp.astype(F32) * (inner - shift)).astype(BF)
    dlog_ref[...] = dlog
    gp = dot(tok, dlog, ((0,), (0,))).reshape(width // 8, 8, n)
    left, right = gp[:, :, :n // 2], gp[:, :, n // 2:]
    even = jnp.where(upper, left, swap_halves(right)).astype(BF)
    odd = jnp.where(upper, swap_halves(left), right).astype(BF)
    all_ref[0] = jnp.where(zero, even, odd).reshape(all_ref.shape[1:])
    all_ref[1] = jnp.where(zero, odd, even).reshape(all_ref.shape[1:])
    here, steps = lax.axis_index("x"), all_ref.shape[1]
    for k in range(steps):
        to = lax.rem(here + k, steps)
        out_refs[k][...] = all_ref[0, to]
        out_refs[steps + k][...] = all_ref[1, to]


def token_outputs(comb_ref, so_ref, dlog_ref, par_ref, dexp_ref, sc_ref, mixed_ref, grad_ref):
    mixed_ref[...] = dot(comb_ref[...], so_ref[...]).astype(BF)
    grad = dot(dlog_ref[...], par_ref[...], ((1,), (1,)))
    grad_ref[...] = (grad + dot(dexp_ref[...], sc_ref[...])).astype(BF)


def add_halves(a_ref, b_ref, out_ref):
    out_ref[...] = (a_ref[...].astype(F32) + b_ref[...].astype(F32)).astype(BF)


def add_rows(own_ref, a_ref, b_ref, c_ref, after_ref, out_ref):
    del after_ref
    pairs = [r[...].astype(F32) for r in (own_ref, a_ref, b_ref, c_ref)]
    out_ref[...] = ((pairs[0] + pairs[1]) + (pairs[2] + pairs[3])).astype(BF)


def sum_pieces(in_ref, out_ref):
    value = in_ref[...].astype(F32)
    count, rows, half = value.shape
    total = jnp.sum(jnp.sum(value.reshape(count // 8, 8, rows, half), axis=0), axis=0)
    out_ref[:, :half] = total[:4]
    out_ref[:, half:] = total[4:]


def shifted(value, step, size, axis="x"):
    return lax.ppermute(value, axis, [(i, (i + step) % size) for i in range(size)])


def on_device(tokens, slot_parameters, w_in, w_out, grad_out):
    shape = jax.ShapeDtypeStruct
    tok, cot = tokens[0], grad_out[0]
    count, width = tok.shape
    n = slot_parameters.shape[1]
    videos = lax.axis_size("x")
    depth, rows_y = lax.axis_size("z"), lax.axis_size("y")
    owners = depth * rows_y
    wide = width + STAT
    unit = 2 * count * width * n
    swap = [(0, 1), (1, 0)]

    vmem = pl.BlockSpec(memory_space=pltpu.VMEM)
    tiles = (depth * (width // STAT) + 1, 8, STAT)
    *blocks, logits = pl.pallas_call(
        reduce_tokens,
        out_shape=[shape(tiles, BF)] * (2 * rows_y) + [shape((count, n), F32)],
        in_specs=[pl.BlockSpec(memory_space=pltpu.HBM)] * 3,
        out_specs=[vmem] * (2 * rows_y + 1),
        scratch_shapes=[
            pltpu.VMEM((count, width), BF), pltpu.VMEM((count, width), BF),
            pltpu.VMEM((width, n), BF), pltpu.VMEM((count, n), BF),
            pltpu.VMEM((2, rows_y) + tiles, BF),
            pltpu.SemaphoreType.DMA((PARTS + 2,)),
        ],
        compiler_params=PARAMS,
        cost_estimate=pl.CostEstimate(flops=4 * unit, bytes_accessed=4 << 20, transcendentals=0),
    )(*[pltpu.with_memory_space_constraint(a, pltpu.HBM) for a in (tok, cot, slot_parameters)])
    order = sorted(range(rows_y), key=lambda k: -min(k, rows_y - k))
    others = {k: lax.ppermute(blocks[rows_y + k], "c", swap) for k in order}
    shares = {}
    for k in order:
        (share,) = call(merge_cores, [shape(tiles, BF)], blocks[k], others[k], flops=10 * unit)
        if k:
            last = share
        shares[k] = shifted(share, k, rows_y, "y") if k else share
    win_t, wout_t = pl.pallas_call(
        turn_weights,
        out_shape=[shape(w_in.shape, BF), shape(w_out.shape, BF)],
        in_specs=[vmem, vmem, pl.BlockSpec(memory_space=pl.ANY)],
        out_specs=[vmem, vmem],
        compiler_params=PARAMS,
        cost_estimate=pl.CostEstimate(flops=20 * unit, bytes_accessed=8 * w_in.size, transcendentals=0),
    )(w_in, w_out, last)
    merged = pl.pallas_call(
        merge_columns,
        out_shape=shape((depth, width // STAT + 1, 8, STAT), BF),
        in_specs=[vmem] * rows_y + [pl.BlockSpec(memory_space=pl.ANY)],
        out_specs=vmem,
        compiler_params=PARAMS,
    )(*[shares[k] for k in range(rows_y)], wout_t)
    shards = lax.all_to_all(merged, "z", 0, 0, tiled=True)
    pay, full, side = call(
        merge_shards,
        [shape((8, width), BF), shape((8, width), F32), shape((8, STAT), F32)],
        shards,
    )
    behind = [shifted(pay, k, videos) for k in range(1, videos)]
    partial = call(
        experts, [shape((8, width), BF)] * videos, pay, *behind, w_in, w_out, win_t, wout_t,
        flops=32 * videos * w_in.size,
    )
    parts = [shifted(partial[k], -k, videos) for k in range(1, videos)]
    (block,) = call(finish_slots, [shape((owners, 4, 2 * width + STAT), BF)], partial[0], *parts, full, side)
    mine = lax.all_to_all(block, ZY, 0, 0, tiled=True)
    theirs = lax.ppermute(mine, "c", swap)

    quarter = shape((owners, 8, n // 2), BF)
    *quarters, dlog, dexp, comb, slot_out, scaled = call(
        token_grads,
        [quarter] * (2 * videos)
        + [shape((count, n), BF), shape((count, n), BF), shape((count, n), BF),
           shape((n, width), BF), shape((n, width), BF)],
        logits, tok, cot, mine, theirs, flops=5 * unit,
        scratch=[pltpu.VMEM((2, videos) + quarter.shape, BF)],
    )
    order = sorted(range(videos), key=lambda k: -min(k, videos - k))
    others = {k: lax.ppermute(quarters[videos + k], "c", swap) for k in order}
    shares = {}
    for k in order:
        (share,) = call(add_halves, [quarter], quarters[k], others[k])
        shares[k] = shifted(share, k, videos) if k else share
    mixed, grad_tokens = call(
        token_outputs,
        [shape((count, width), BF), shape((count, width), BF)],
        comb, slot_out, dlog, slot_parameters, dexp, scaled, flops=3 * unit,
    )
    half = pl.pallas_call(
        add_rows,
        out_shape=quarter,
        in_specs=[vmem] * videos + [pl.BlockSpec(memory_space=pltpu.HBM)],
        out_specs=vmem,
        compiler_params=PARAMS,
    )(*[shares[k] for k in range(videos)], pltpu.with_memory_space_constraint(mixed, pltpu.HBM))
    pieces = lax.all_to_all(half, ZY, 0, 0, tiled=True)
    (grad_params,) = call(sum_pieces, [shape((4, n), F32)], pieces)
    return mixed[None], grad_tokens[None], grad_params


def solution(mesh):
    sizes = dict(mesh.shape)
    grid = Mesh(mesh.devices.reshape(sizes["batch"], sizes["seq"] // 8, 4, 2), AXES)
    seq = ("z", "y", "c")
    placed = (
        P("x", seq, None),
        P(),
        P(seq, None, "x"),
        P(seq, "x", None),
        P("x", seq, None),
    )
    return jax.shard_map(
        on_device,
        mesh=grid,
        in_specs=placed,
        out_specs=(P("x", seq, None), P("x", seq, None), P(AXES, None)),
        check_vma=False,
    )
```
